32 devices in a mesh: wide: 8 (over z, y), narrow: 4 (over x, core).
Axes of the slice: x: 2, y: 2, z: 4, core: 2. Of those that a mesh axis runs over, the one named last changes fastest.
Arguments:
- tokens: bfloat16 [16384, 768], P(('wide', 'narrow')), may hold values from -6 to 6
- skip_tokens: bfloat16 [16384, 768], P(('wide', 'narrow')), may hold values from -6 to 6
- cot_first: bfloat16 [16384, 768], P(('wide', 'narrow')), may hold values from -6 to 6
- cot_second: bfloat16 [16384, 768], P(('wide', 'narrow')), may hold values from -6 to 6
- w_qkv: bfloat16 [2, 768, 2304], P(None, None, ('wide', 'narrow')), may hold values from -0.21875 to 0.21875
- w_out: bfloat16 [2, 768, 768], P(None, None, ('wide', 'narrow')), may hold values from -1.75 to 1.75
- w_up: bfloat16 [2, 768, 3072], P(None, None, ('wide', 'narrow')), may hold values from -0.21875 to 0.21875
- w_down: bfloat16 [2, 3072, 768], P(None, ('wide', 'narrow')), may hold values from -0.109375 to 0.109375
- biases: bfloat16 [2, 6, 768], P(None, None, ('wide', 'narrow')), may hold values from -0.59765625 to 0.59765625
- norm_gains: bfloat16 [2, 2, 768], P(None, None, ('wide', 'narrow')), may hold values from 0.5 to 1.5
- up_bias: bfloat16 [2, 3072], P(None, ('wide', 'narrow')), may hold values from -0.59765625 to 0.59765625
- lengths: int32 [32], P(('wide', 'narrow')), may hold values from 409 to 512
- segments: int32 [32, 512], P(('wide', 'narrow')), may hold values from 0 to 7, never falling along the last dimension, each value on 1 to 128 neighbouring positions
Outputs:
- out_first: bfloat16 [16384, 768], P(('wide', 'narrow'))
- out_second: bfloat16 [16384, 768], P(('wide', 'narrow'))
- grad_tokens: float32 [16384, 768], P(('wide', 'narrow'))
- grad_skip: float32 [16384, 768], P(('wide', 'narrow'))
- grad_w_qkv: float32 [2, 768, 2304], P(None, None, ('wide', 'narrow'))
- grad_w_out: float32 [2, 768, 768], P(None, None, ('wide', 'narrow'))
- grad_w_up: float32 [2, 768, 3072], P(None, None, ('wide', 'narrow'))
- grad_w_down: float32 [2, 3072, 768], P(None, ('wide', 'narrow'))
- grad_biases: float32 [2, 6, 768], P(None, None, ('wide', 'narrow'))
- grad_gains: float32 [2, 2, 768], P(None, None, ('wide', 'narrow'))
- grad_up_bias: float32 [2, 3072], P(None, ('wide', 'narrow'))
The draws below stay inside these ranges and needn't reach their ends.
All inputs are finite; a program needn't handle non-finite values.
Results may differ from the reference program's by a relative error of at most 0.017.
Values may be sent and summed in bfloat16 or wider, within the bound.
No kernel may reach another device: no remote copies, remote signals or barrier semaphores. Data moves between devices by JAX's collectives and lax.ppermute only.
A program may use at most 256 MiB of HBM per device.

```python
import math
import jax
import jax.numpy as jnp
import numpy as np
from jax import lax

D = 768
HEADS = 12
HEAD_DIM = 64
FF = 3072
SEQ_LEN = 512
DOCS = 8
SEQS = 32
TOKENS = 16384


def set_ends(result, key, low, high):
    place = [jax.random.randint(jax.random.fold_in(key, axis), (), 0, length) for axis, length in enumerate(result.shape)]
    main_axis = result.shape.index(max(result.shape))
    next_to = place[:main_axis] + [(place[main_axis] + 1) % result.shape[main_axis]] + place[main_axis + 1:]
    return result.at[tuple(place)].set(low).at[tuple(next_to)].set(high)


def spiked(entries, stream_key, source, target, blocks, factor):
    owner, partner = [(jnp.arange(entries.shape[dim]) // (entries.shape[dim] // blocks)).reshape([-1 if axis == dim else 1 for axis in range(entries.ndim)]) for dim in (source, target)]
    chosen = jax.random.permutation(stream_key, blocks)[partner]
    strong = (owner == chosen) | (owner == (partner + blocks // 2) % blocks)
    return jnp.where(strong, factor * entries, entries)


def levels(rng, shape, split, smallest, high):
    gain, own = 1.0, jax.random.fold_in(rng, 6)
    for dim, parts in split:
        heights = jnp.exp(jax.random.uniform(jax.random.fold_in(own, dim), (parts,), jnp.float32, smallest / len(split), high / len(split)))
        gain = gain * jnp.repeat(heights, shape[dim] // parts).reshape([-1 if axis == dim else 1 for axis in range(len(shape))])
    return gain


def profile(number_of, total, bound, lean):
    weights = [(1 << 20) // math.isqrt(standing ** lean) + 1 for standing in range(2, number_of + 1)]
    surplus, counts = total - bound - (number_of - 1), [1] * (number_of - 1)
    while surplus > 0:
        movable = [i for i in range(number_of - 1) if counts[i] < bound]
        pool, budget = sum([weights[i] for i in movable]), surplus
        for i in movable:
            more = min(bound - counts[i], max(1, budget * weights[i] // pool), surplus)
            counts[i] = counts[i] + more
            surplus = surplus - more
    return np.array([bound] + counts)


def ragged(own_key, amount, total, limit, slope):
    if amount == 2:
        one = jax.random.randint(own_key, (), max(1, total - limit), min(limit, total - 1) + 1)
        return jnp.stack([one, total - one])
    sizes = jnp.asarray(profile(amount, total, limit, slope), jnp.int32)
    couples = (amount - 1) // 2
    giver, receiver = sizes[1:1 + 2 * couples:2], sizes[2:2 + 2 * couples:2]
    slack = jnp.minimum(giver - 1, limit - receiver)
    moved = jax.random.randint(jax.random.fold_in(own_key, 1), (couples,), 0, 1 << 20) % (slack + 1)
    sizes = sizes.at[1:1 + 2 * couples:2].set(giver - moved).at[2:2 + 2 * couples:2].set(receiver + moved)
    return sizes[jax.random.permutation(jax.random.fold_in(own_key, 2), amount)]


def normal_values(stream_key, dims, spread, most, cuts=(), dtype=jnp.bfloat16):
    values = jax.random.normal(stream_key, dims, jnp.float32) * spread
    if len(cuts) > 0:
        values = levels(stream_key, dims, cuts, -0.22, 0.18) * values
    return jnp.clip(values, min=-most, max=most).astype(dtype)


def noise_with(own_key, dims, scale, most, shards, heavy, kind=jnp.bfloat16):
    result = scale * jax.random.normal(own_key, dims, jnp.float32)
    if shards:
        result = result * levels(own_key, dims, shards, -0.22, 0.18)
    return jnp.clip(spiked(result, jax.random.fold_in(own_key, 3), *heavy), -most, most).astype(kind)


def setup_inputs(seed: int = 0) -> dict:
    key_of = jax.random.split(jax.random.key(seed), 14)
    tokens = noise_with(key_of[0], (TOKENS, D), 1.0, 6.0, ((0, 32),), (0, 1, 32, 2.75))
    skip_tokens = noise_with(key_of[1], (TOKENS, D), 1.0, 6.0, ((0, 32),), (0, 1, 32, 2.75))
    cot_first = noise_with(key_of[2], (TOKENS, D), 1.0, 6.0, ((0, 32),), (0, 1, 32, 2.75))
    cot_second = noise_with(key_of[3], (TOKENS, D), 1.0, 6.0, ((0, 32),), (0, 1, 32, 2.75))
    w_qkv = normal_values(key_of[4], (2, D, 3 * D), D ** -0.5, 0.21875, ((2, 32),))
    w_out = normal_values(key_of[5], (2, D, D), (D // 64) ** -0.5, 1.75, ((2, 32),))
    w_up = normal_values(key_of[6], (2, D, FF), D ** -0.5, 0.21875, ((2, 32),))
    w_down = normal_values(key_of[7], (2, FF, D), FF ** -0.5, 0.109375, ((1, 32),))
    biases = normal_values(key_of[8], (2, 6, D), 0.1, 0.59765625, ((2, 32),))
    norm_gains = jnp.clip(1.0 + 0.1 * jax.random.normal(key_of[9], (2, 2, D), jnp.float32), 0.5, 1.5).astype(jnp.bfloat16)
    up_bias = normal_values(key_of[10], (2, FF), 0.1, 0.59765625, ((1, 32),))
    lengths = set_ends(jax.random.randint(key_of[11], (SEQS,), SEQ_LEN * 4 // 5, SEQ_LEN + 1), jax.random.fold_in(key_of[11], 1), SEQ_LEN * 4 // 5, SEQ_LEN).astype(jnp.int32)
    segments = jax.vmap(lambda own: jnp.searchsorted(jnp.cumsum(ragged(own, DOCS, SEQ_LEN, SEQ_LEN // 4, 0)), jnp.arange(SEQ_LEN), side="right"))(jax.random.split(key_of[12], SEQS)).reshape((SEQS, SEQ_LEN)).astype(jnp.int32)
    return dict(tokens=tokens, skip_tokens=skip_tokens, cot_first=cot_first, cot_second=cot_second, w_qkv=w_qkv, w_out=w_out, w_up=w_up, w_down=w_down, biases=biases, norm_gains=norm_gains, up_bias=up_bias, lengths=lengths, segments=segments)


EPSILON = 1e-12
MASKED = -1e+30
HIGHEST = lax.Precision.HIGHEST

@jax.custom_vjp
def low(v):
    return lax.optimization_barrier(v.astype(jnp.bfloat16)).astype(jnp.float32)

@jax.custom_vjp
def low_back(v):
    return v

def low_keep(v):
    return (low(v), None)

def low_pass(kept, grad):
    return (grad,)

def back_keep(v):
    return (v, None)

def back_low(kept, grad):
    return (low(grad),)
low.defvjp(low_keep, low_pass)
low_back.defvjp(back_keep, back_low)

def layer_norm(values, norm_gain, norm_shift):
    average = lax.optimization_barrier(jnp.mean(values, -1, keepdims=True))
    centred = values - average
    return centred * lax.rsqrt(lax.optimization_barrier(jnp.mean(centred * centred, -1, keepdims=True)) + EPSILON) * norm_gain + norm_shift

def allowed(lengths, segments):
    position = lax.broadcasted_iota(jnp.int32, segments.shape, 1)
    living = position < lengths[:, None]
    same_doc = segments[:, :, None] == segments[:, None, :]
    itself = position[:, :, None] == position[:, None, :]
    return same_doc & living[:, None, :] | itself

def block(hidden, w_qkv, w_out, w_up, w_down, bias_rows, gain_rows, up_bias, allowed_mask):
    group_seqs = allowed_mask.shape[0]
    row_count = hidden.shape[0]
    no_bias = jnp.zeros((D,), jnp.float32)
    projected = jnp.dot(hidden, w_qkv, precision=HIGHEST) + jnp.concatenate([bias_rows[0], no_bias, bias_rows[1]])
    projected = low_back(low(projected))
    split_heads = projected.reshape(group_seqs, SEQ_LEN, 3, HEADS, HEAD_DIM)
    queries = split_heads[:, :, 0]
    keys_in = split_heads[:, :, 1]
    values_in = split_heads[:, :, 2]
    scores = jnp.einsum('gqhe,gkhe->ghqk', queries, keys_in, precision=HIGHEST) * HEAD_DIM ** (-0.5)
    scores = low_back(jnp.where(allowed_mask[:, None], scores, MASKED))
    probs_low = low(jax.nn.softmax(scores, axis=-1))
    mixed_heads = jnp.einsum('ghqk,gkhe->gqhe', probs_low, values_in, precision=HIGHEST)
    mixed_heads = low_back(low(mixed_heads.reshape(row_count, D)))
    branch = low_back(jnp.dot(mixed_heads, w_out, precision=HIGHEST) + bias_rows[2])
    first_norm = low(layer_norm(hidden + branch, gain_rows[0], bias_rows[4]))
    upper_in = low_back(jnp.dot(first_norm, w_up, precision=HIGHEST) + up_bias)
    active = low(jax.nn.gelu(upper_in, approximate=False))
    lower_out = low_back(jnp.dot(active, w_down, precision=HIGHEST) + bias_rows[3])
    return layer_norm(first_norm + lower_out, gain_rows[1], bias_rows[5])

def forward(tokens, skip_tokens, params, allowed_mask):
    w_qkv, w_out, w_up, w_down, biases, norm_gains, up_bias = params
    out_first = low(block(tokens, w_qkv[0], w_out[0], w_up[0], w_down[0], biases[0], norm_gains[0], up_bias[0], allowed_mask))
    group_seqs = allowed_mask.shape[0]
    is_first = (lax.broadcasted_iota(jnp.int32, (group_seqs, SEQ_LEN, 1), 1) == 0).reshape(group_seqs * SEQ_LEN, 1)
    second_in = jnp.where(is_first, out_first, skip_tokens)
    out_second = low(block(second_in, w_qkv[1], w_out[1], w_up[1], w_down[1], biases[1], norm_gains[1], up_bias[1], allowed_mask))
    return (out_first, out_second)

def reference(tokens, skip_tokens, cot_first, cot_second, w_qkv, w_out, w_up, w_down, biases, norm_gains, up_bias, lengths, segments):
    group_seqs = math.gcd(SEQS, 8)
    rounds = SEQS // group_seqs
    row_count = group_seqs * SEQ_LEN
    params = tuple((parameter.astype(jnp.float32) for parameter in (w_qkv, w_out, w_up, w_down, biases, norm_gains, up_bias)))

    def shaped(array):
        return array.astype(jnp.float32).reshape(rounds, row_count, D)

    def one_group(running, inputs_one):
        token_rows, skip_rows, first_cot, second_cot, length_rows, segment_rows = inputs_one
        allowed_mask = allowed(length_rows, segment_rows)

        def apply_both(token_arg, skip_arg, *param_args):
            return forward(token_arg, skip_arg, param_args, allowed_mask)
        outputs, pullback = jax.vjp(apply_both, token_rows, skip_rows, *params)
        gradients = pullback((first_cot, second_cot))
        running = tuple((partial_sum + gradient for partial_sum, gradient in zip(running, gradients[2:])))
        return (running, (outputs[0], outputs[1], gradients[0], gradients[1]))
    initial = tuple((jnp.zeros(parameter.shape, jnp.float32) for parameter in params))
    sums, per_group = lax.scan(one_group, initial, (shaped(tokens), shaped(skip_tokens), shaped(cot_first), shaped(cot_second), lengths.reshape(rounds, group_seqs), segments.reshape(rounds, group_seqs, SEQ_LEN)))
    out_first = per_group[0].reshape(TOKENS, D).astype(jnp.bfloat16)
    out_second = per_group[1].reshape(TOKENS, D).astype(jnp.bfloat16)
    grad_tokens = per_group[2].reshape(TOKENS, D)
    grad_skip = per_group[3].reshape(TOKENS, D)
    return (out_first, out_second, grad_tokens, grad_skip, sums[0], sums[1], sums[2], sums[3], sums[4], sums[5], sums[6])
```

```python
import functools
import math

import jax
import jax.numpy as jnp
from jax import lax
from jax.experimental import pallas as pl
from jax.experimental.pallas import tpu as pltpu
from jax.sharding import Mesh, PartitionSpec as P

HEADS = 12
HEAD_DIM = 64
EPSILON = 1e-12
MASKED = -1e30
BF = jnp.bfloat16
F32 = jnp.float32
NT = (((1,), (1,)), ((), ()))
TN = (((0,), (0,)), ((), ()))
NN = (((1,), (0,)), ((), ()))
PARTS = 8
LANES = 128
VMEM = pl.BlockSpec(memory_space=pltpu.VMEM)


def mm(a, b, dims=NN):
    return lax.dot_general(a, b, dims, preferred_element_type=F32)


def call(kernel, out_shapes, scratch, flops, *args):
    n_bytes = sum(a.size * a.dtype.itemsize for a in args) + sum(
        math.prod(o.shape) * jnp.dtype(o.dtype).itemsize for o in out_shapes
    )
    return pl.pallas_call(
        kernel,
        out_shape=out_shapes,
        in_specs=[VMEM] * len(args),
        out_specs=[VMEM] * len(out_shapes),
        scratch_shapes=scratch,
        compiler_params=pltpu.CompilerParams(vmem_limit_bytes=56 * 1024 * 1024),
        cost_estimate=pl.CostEstimate(flops=flops, bytes_accessed=n_bytes, transcendentals=0),
    )(*args)


def windows(length):
    tiles = length // LANES
    return [
        (t, max(0, t - 1) * LANES, min(tiles, t + 2) * LANES) for t in range(tiles)
    ]


def attention_forward_kernel(length, width, x, wt, bias, seg_col, key_row, qkv, mix, lse_rows, mask, lse):
    for part in range(3):
        cols = slice(part * width, (part + 1) * width)
        qkv[:, cols] = (mm(x[...], wt[cols, :], NT) + bias[:, cols]).astype(BF)
    for t, low, high in windows(length):
        rows = lax.broadcasted_iota(jnp.int32, (LANES, high - low), 0) + t * LANES
        keys = lax.broadcasted_iota(jnp.int32, (LANES, high - low), 1) + low
        same = seg_col[t * LANES : (t + 1) * LANES, :] == key_row[:, low:high]
        mask[t, :, : high - low] = jnp.where(same | (rows == keys), 0.0, MASKED)
    lse[...] = jnp.zeros_like(lse)

    def pair(p, carry):
        at = pl.multiple_of(p * LANES, LANES)
        lane = lax.broadcasted_iota(jnp.int32, (LANES, LANES), 1)
        for t, low, high in windows(length):
            here = slice(t * LANES, (t + 1) * LANES)
            q = qkv[here, pl.ds(at, LANES)] * HEAD_DIM ** (-0.5)
            k = qkv[low:high, pl.ds(pl.multiple_of(at + width, LANES), LANES)]
            v = qkv[low:high, pl.ds(pl.multiple_of(at + 2 * width, LANES), LANES)]
            outs = []
            for h in range(2):
                mine = (lane < HEAD_DIM) == (h == 0)
                s = mm(jnp.where(mine, q, 0).astype(BF), k, NT) + mask[t, :, : high - low]
                top = jnp.max(s, -1, keepdims=True)
                e = jnp.exp(s - top)
                total = jnp.sum(e, -1, keepdims=True)
                outs.append(mm((e * (1.0 / total)).astype(BF), v))
                lse[here, :] = jnp.where(lane == 2 * p + h, top + jnp.log(total), lse[here, :])
            mix[here, pl.ds(at, LANES)] = jnp.where(lane < HEAD_DIM, outs[0], outs[1]).astype(BF)
        return carry

    lax.fori_loop(0, width // LANES, pair, 0)
    lse_rows[...] = lse[...].T[: lse_rows.shape[0], :]


def attention_forward(x, wt, bias, seg_col, key_row):
    length, width = x.shape
    shapes = [
        jax.ShapeDtypeStruct((length, 3 * width), BF),
        jax.ShapeDtypeStruct((length, width), BF),
        jax.ShapeDtypeStruct((16, length), F32),
    ]
    scratch = [
        pltpu.VMEM((length // LANES, LANES, 3 * LANES), F32),
        pltpu.VMEM((length, LANES), F32),
    ]
    flops = 2 * length * width * 3 * width + 4 * 4 * length * length * width
    return call(
        functools.partial(attention_forward_kernel, length, width),
        shapes, scratch, flops, x, wt, bias, seg_col, key_row,
    )


def attention_backward_kernel(length, width, qkv, dmix, mix, lse_rows, seg_row, key_col, dqkv, sums, mask, dq_sum):
    for t, low, high in windows(length):
        keys = lax.broadcasted_iota(jnp.int32, (LANES, high - low), 0) + t * LANES
        rows = lax.broadcasted_iota(jnp.int32, (LANES, high - low), 1) + low
        same = key_col[t * LANES : (t + 1) * LANES, :] == seg_row[:, low:high]
        mask[t, :, : high - low] = jnp.where(same | (rows == keys), 0.0, MASKED)

    def pair(p, carry):
        at = pl.multiple_of(p * LANES, LANES)
        at_k = pl.multiple_of(at + width, LANES)
        at_v = pl.multiple_of(at + 2 * width, LANES)
        lane = lax.broadcasted_iota(jnp.int32, (length, LANES), 1)
        q = qkv[:, pl.ds(at, LANES)] * HEAD_DIM ** (-0.5)
        dm = dmix[:, pl.ds(at, LANES)]
        product = dm.astype(F32) * mix[:, pl.ds(at, LANES)].astype(F32)
        ones_lane = lax.broadcasted_iota(jnp.int32, (8, LANES), 1)
        q_h, dm_h, lse_h, delta_h = [], [], [], []
        for h in range(2):
            mine = (lane < HEAD_DIM) == (h == 0)
            q_h.append(jnp.where(mine, q, 0).astype(BF))
            dm_h.append(jnp.where(mine, dm, 0).astype(BF))
            picks = jnp.where((ones_lane < HEAD_DIM) == (h == 0), 1.0, 0.0)
            delta_h.append(
                lax.dot_general(picks, product, NT, precision=lax.Precision.HIGHEST, preferred_element_type=F32)[:1, :]
            )
            lse_h.append(lse_rows[pl.ds(2 * p + h, 1), :])
        dq_sum[...] = jnp.zeros_like(dq_sum)
        for t, low, high in windows(length):
            here = slice(t * LANES, (t + 1) * LANES)
            k = qkv[here, pl.ds(at_k, LANES)]
            v = qkv[here, pl.ds(at_v, LANES)]
            dk = jnp.zeros((LANES, LANES), F32)
            dv = jnp.zeros((LANES, LANES), F32)
            dq = jnp.zeros((high - low, LANES), F32)
            for h in range(2):
                mine = (lane[:LANES] < HEAD_DIM) == (h == 0)
                q_one, dm_one = q_h[h][low:high], dm_h[h][low:high]
                s = mm(k, q_one, NT) + mask[t, :, : high - low]
                a = jnp.exp(s - lse_h[h][:, low:high])
                da = mm(v, dm_one, NT)
                ds = (a * (da - delta_h[h][:, low:high])).astype(BF)
                dv += mm(a.astype(BF), dm_one)
                dk += mm(ds, q_one)
                dq += mm(ds, jnp.where(mine, k, 0).astype(BF), TN)
            dqkv[here, pl.ds(at_k, LANES)] = dk.astype(BF)
            dqkv[here, pl.ds(at_v, LANES)] = dv.astype(BF)
            dq_sum[low:high, :] += dq
        dqkv[:, pl.ds(at, LANES)] = (dq_sum[...] * HEAD_DIM ** (-0.5)).astype(BF)
        return carry

    lax.fori_loop(0, width // LANES, pair, 0)
    for part in range(3):
        cols = slice(part * width, (part + 1) * width)
        sums[:, cols] = mm(jnp.ones((8, length), BF), dqkv[:, cols])


def attention_backward(qkv, dmix, mix, lse_rows, seg_row, key_col):
    length, width = mix.shape
    shapes = [
        jax.ShapeDtypeStruct((length, 3 * width), BF),
        jax.ShapeDtypeStruct((8, 3 * width), F32),
    ]
    scratch = [
        pltpu.VMEM((length // LANES, LANES, 3 * LANES), F32),
        pltpu.VMEM((length, LANES), F32),
    ]
    flops = 10 * 4 * length * length * width
    return call(
        functools.partial(attention_backward_kernel, length, width),
        shapes, scratch, flops, qkv, dmix, mix, lse_rows, seg_row, key_col,
    )


def norm(values):
    centred = values - jnp.mean(values, -1, keepdims=True)
    inverse = lax.rsqrt(jnp.mean(centred * centred, -1, keepdims=True) + EPSILON)
    return centred * inverse, inverse


def norm_back(upstream, scaled, inverse, gain):
    through = upstream * gain
    return inverse * (
        through
        - jnp.mean(through, -1, keepdims=True)
        - scaled * jnp.mean(through * scaled, -1, keepdims=True)
    )


def normal_terms(u):
    size = jnp.abs(u) * (1.0 / math.sqrt(2.0))
    bell = jnp.exp(-(size * size))
    s = 1.0 / (1.0 + 0.3275911 * size)
    tail = s * (0.5 * 0.254829592 + s * (0.5 * -0.284496736 + s * (0.5 * 1.421413741 + s * (0.5 * -1.453152027 + s * (0.5 * 1.061405429)))))
    tail = tail * bell
    return jnp.where(u > 0, 1.0 - tail, tail), bell * (1.0 / math.sqrt(2.0 * math.pi))


def feed_kernel(layout, backward, tile, *refs):
    refs = list(refs)
    take = lambda n: [refs.pop(0) for _ in range(n)]
    x, mix, w_out, vectors, up_bias = take(5)
    (cot,) = take(1) if backward else (None,)
    pieces = [take(n) for n in layout]
    if backward:
        y, n1_out, g_out, du_out, df_out, do_out, dr1_out, dm_out, small, up_small, slope = refs
        small[...] = jnp.zeros_like(small)
        up_small[...] = jnp.zeros_like(up_small)
    else:
        (y,) = refs
    count, width = x.shape

    def weights(part, lower):
        got = []
        for ref in pieces[part]:
            half = ref.shape[1] // 2
            block = ref[:, half:, :] if lower else ref[:, :half, :]
            got.append(block.reshape(ref.shape[0] * half, width))
        return got[0] if len(got) == 1 else jnp.concatenate(got, 0)

    b_out, b_down, shift_one, shift_two, gain_one, gain_two = (vectors[i : i + 1, :] for i in range(6))

    def rows_step(i, carry):
        rows = pl.ds(pl.multiple_of(i * tile, tile), tile)
        r1 = x[rows, :].astype(F32) + mm(mix[rows, :], w_out[...], NT) + b_out
        z1, q1 = norm(r1)
        n1 = (z1 * gain_one + shift_one).astype(BF)
        acc = n1.astype(F32) + b_down
        for part in range(PARTS):
            u = mm(n1, weights(part, False), NT) + up_bias[part : part + 1, :]
            size = u.shape[1]
            cols = slice(part * size, (part + 1) * size)
            big, bell = normal_terms(u)
            g = (u * big).astype(BF)
            if backward:
                g_out[rows, cols] = g
                slope[:, cols] = big + u * bell
            acc += mm(g, weights(part, True))
        z2, q2 = norm(acc)
        y[rows, :] = (z2 * gain_two + shift_two).astype(BF)
        if backward:
            e = cot[rows, :].astype(F32)
            small[3:4, :] += jnp.sum(e, 0, keepdims=True)
            small[5:6, :] += jnp.sum(e * z2, 0, keepdims=True)
            dr2 = norm_back(e, z2, q2, gain_two)
            df = dr2.astype(BF)
            small[1:2, :] += jnp.sum(df.astype(F32), 0, keepdims=True)
            dn1 = dr2
            for part in range(PARTS):
                da = mm(df, weights(part, True), NT)
                size = da.shape[1]
                cols = slice(part * size, (part + 1) * size)
                du = (da * slope[:, cols]).astype(BF)
                du_out[rows, cols] = du
                up_small[part : part + 1, :] += jnp.sum(du.astype(F32), 0, keepdims=True)
                dn1 += mm(du, weights(part, False))
            small[2:3, :] += jnp.sum(dn1, 0, keepdims=True)
            small[4:5, :] += jnp.sum(dn1 * z1, 0, keepdims=True)
            dr1 = norm_back(dn1, z1, q1, gain_one)
            do = dr1.astype(BF)
            small[0:1, :] += jnp.sum(do.astype(F32), 0, keepdims=True)
            dm_out[rows, :] = mm(do, w_out[...]).astype(BF)
            n1_out[rows, :] = n1
            df_out[rows, :] = df
            do_out[rows, :] = do
            dr1_out[rows, :] = dr1
        return carry

    lax.fori_loop(0, count // tile, rows_step, 0)


def feed(x, mix, w_out, vectors, up_bias, pieces, cot=None):
    count, width = x.shape
    hidden = PARTS * up_bias.shape[1]
    tile = min(256, count)
    backward = cot is not None
    wide = jax.ShapeDtypeStruct((count, width), BF)
    high = jax.ShapeDtypeStruct((count, hidden), BF)
    shapes, scratch = [wide], []
    args = [x, mix, w_out, vectors, up_bias]
    if backward:
        args.append(cot)
        shapes += [
            wide, high, high, wide, wide, jax.ShapeDtypeStruct((count, width), F32), wide,
            jax.ShapeDtypeStruct((8, width), F32), jax.ShapeDtypeStruct(up_bias.shape, F32),
        ]
        scratch.append(pltpu.VMEM((tile, hidden), F32))
    layout = [len(piece) for piece in pieces]
    flops = 4 * count * width * (hidden + width) * (2 if backward else 1)
    return call(
        functools.partial(feed_kernel, layout, backward, tile),
        shapes, scratch, flops, *args, *[ref for piece in pieces for ref in piece],
    )


def feed_grads_kernel(first, layout, received, n1, df, g, du, *refs):
    refs = list(refs)
    got = [refs.pop(0) for _ in range(received)]
    for index, sizes in enumerate(layout):
        outs = [refs.pop(0) for _ in sizes]
        size = g.shape[1] // PARTS
        cols = slice((first + index) * size, (first + index + 1) * size)
        for lower, (left, right) in enumerate(((du, n1), (g, df))):
            full = mm(left[:, cols], right[...], TN)
            at = 0
            for out, slabs in zip(outs, sizes):
                half = out.shape[1] // 2
                rows = slice(lower * half, (lower + 1) * half)
                value = full[at * half : (at + slabs) * half].reshape(slabs, half, out.shape[2])
                if received:
                    value += got[0][index, at : at + slabs, rows, :].astype(F32)
                out[:, rows, :] = value.astype(BF)
                at += slabs


def feed_grads(first, layout, half, n1, df, g, du, *received):
    width = n1.shape[1]
    shapes = [jax.ShapeDtypeStruct((slabs, 2 * half, width), BF) for sizes in layout for slabs in sizes]
    flops = 4 * n1.shape[0] * width * g.shape[1] // 2
    return call(
        functools.partial(feed_grads_kernel, first, layout, len(received)),
        shapes, [], flops, n1, df, g, du, *received,
    )


class Near:
    axes = ("z", "y", "x", "core")
    feed_layout = [1, 1, 1, 2] * 2

    def __init__(self):
        self.at = {name: lax.axis_index(name) for name in self.axes}
        self.z = lax.axis_size("z")

    def swap(self, array, axis):
        return lax.ppermute(array, axis, [(0, 1), (1, 0)])

    def gather(self, slab):
        half = self.z // 2
        here = lax.all_gather(slab, "z", axis=0, tiled=False)
        by_y, by_x = self.swap(here, "y"), self.swap(here, "x")
        both = [self.swap(by_y[:half], "x"), self.swap(by_x[half:], "y")]
        own = [here, by_y, by_x, *both]
        return own, [self.swap(part, "core") for part in own]

    def gather_feed(self, slab):
        own, other = self.gather(slab)
        return [[p[0]] for p in []] + [[own[0]], [own[1]], [own[2]], own[3:], [other[0]], [other[1]], [other[2]], other[3:]]

    def place(self, core, y, x):
        return (core ^ self.at["core"]) * 4 + (y ^ self.at["y"]) * 2 + (x ^ self.at["x"])

    def gather_attention(self, slab):
        own, other = self.gather(slab)
        parts = jnp.stack([p for side in (own, other) for p in (side[0], side[2], side[1], jnp.concatenate(side[3:], 0))])
        order = [
            lax.dynamic_index_in_dim(parts, self.place(core, y, x), 0, keepdims=False)
            for y in range(2) for x in range(2) for core in range(2)
        ]
        return jnp.stack(order, 1).reshape((-1,) + slab.shape)

    def relative(self, natural):
        blocks = natural.reshape((self.z, 8) + natural.shape[1:])
        out = []
        for core in range(2):
            for y, x in ((0, 0), (1, 0), (0, 1), (1, 1)):
                index = (y ^ self.at["y"]) * 4 + (x ^ self.at["x"]) * 2 + (core ^ self.at["core"])
                out.append(lax.dynamic_index_in_dim(blocks, index, 1, keepdims=False))
        return out

    def up_bias(self, natural):
        return jnp.stack(self.relative(natural)).reshape(PARTS, -1)

    def up_bias_grad(self, parts):
        blocks = parts.reshape(PARTS, self.z, -1)
        order = []
        for y in range(2):
            for x in range(2):
                for core in range(2):
                    index = (core ^ self.at["core"]) * 4 + (y ^ self.at["y"]) + (x ^ self.at["x"]) * 2
                    order.append(lax.dynamic_index_in_dim(blocks, index, 0, keepdims=False))
        return jnp.stack(order, 1).reshape(self.z * 8, -1)

    def reduce(self, here, by_y, by_x, both_a, both_b):
        half = self.z // 2
        got_a, got_b = self.swap(both_a, "x"), self.swap(both_b, "y")
        by_y = by_y.at[:half].add(got_a)
        by_x = by_x.at[half:].add(got_b)
        total = here + self.swap(by_y, "y") + self.swap(by_x, "x")
        return lax.psum_scatter(total, "z", scatter_dimension=0, tiled=False)

    def reduce_feed(self, n1, df, g, du, half):
        z = self.z
        sent = feed_grads(4, [[z]] * 4, half, n1, df, g, du)
        received = self.swap(jnp.stack(sent), "core")
        return self.reduce(*feed_grads(0, [[z], [z], [z], [z // 2, z // 2]], half, n1, df, g, du, received))

    def reduce_attention(self, slabs):
        parts = self.relative(slabs)
        received = self.swap(jnp.stack(parts[4:]), "core")
        here, by_y, by_x, both = (parts[i] + received[i] for i in range(4))
        half = self.z // 2
        return self.reduce(here, by_y, by_x, both[:half], both[half:])


class Far:
    axes = ("wide", "narrow")
    feed_layout = [1] * PARTS

    def gather_attention(self, slab):
        return lax.all_gather(slab, self.axes, axis=0, tiled=False)

    def gather_feed(self, slab):
        whole = lax.all_gather(slab, self.axes, axis=0, tiled=False)
        half, width = slab.shape[0] // 2, slab.shape[1]
        up = whole[:, :half].reshape(PARTS, -1, width)
        down = whole[:, half:].reshape(PARTS, -1, width)
        both = jnp.concatenate([up, down], 1)
        return [[both[i : i + 1]] for i in range(PARTS)]

    def up_bias(self, natural):
        return natural.reshape(PARTS, -1)

    def up_bias_grad(self, parts):
        return parts.reshape(lax.axis_size("wide") * lax.axis_size("narrow"), -1)

    def reduce_attention(self, slabs):
        return lax.psum_scatter(slabs, self.axes, scatter_dimension=0, tiled=False)

    def reduce_feed(self, n1, df, g, du, half):
        devices = lax.axis_size("wide") * lax.axis_size("narrow")
        rows = g.shape[1] // PARTS
        width = n1.shape[1]
        parts = feed_grads(0, [[1]] * 4, rows, n1, df, g, du) + feed_grads(4, [[1]] * 4, rows, n1, df, g, du)
        both = jnp.concatenate(parts, 0)
        up = both[:, :rows].reshape(devices, half, width)
        down = both[:, rows:].reshape(devices, half, width)
        return lax.psum_scatter(jnp.concatenate([up, down], 1), self.axes, scatter_dimension=0, tiled=False)


SMALL_ROWS = 8


class Block:
    def __init__(self, link, shards, index):
        w_qkv, w_out, w_up, w_down, biases, gains, up_bias = (s[index] for s in shards)
        self.link = link
        self.sizes = (w_qkv.shape[1], w_out.shape[1], up_bias.shape[0])
        width = w_qkv.shape[0]
        small = jnp.concatenate([biases.reshape(-1), gains.reshape(-1), up_bias])
        small = jnp.pad(small, (0, SMALL_ROWS * width - small.shape[0])).reshape(SMALL_ROWS, width)
        self.attention_slab = jnp.concatenate([w_qkv.T, w_out.T, small], 0)
        self.feed_slab = jnp.concatenate([w_up.T, w_down], 0)

    def fetch(self):
        n_qkv, n_out, n_up = self.sizes
        slabs = self.link.gather_attention(self.attention_slab)
        devices, _, width = slabs.shape
        self.wt_qkv = slabs[:, :n_qkv].reshape(devices * n_qkv, width)
        self.wt_out = slabs[:, n_qkv : n_qkv + n_out].reshape(devices * n_out, width)
        small = slabs[:, n_qkv + n_out :].reshape(devices, -1).astype(F32)
        own = width // devices
        biases = small[:, : 6 * own].reshape(devices, 6, own).transpose(1, 0, 2).reshape(6, width)
        gains = small[:, 6 * own : 8 * own].reshape(devices, 2, own).transpose(1, 0, 2).reshape(2, width)
        self.up_bias = self.link.up_bias(small[:, 8 * own : 8 * own + n_up])
        self.qkv_bias = jnp.concatenate([biases[0], jnp.zeros((width,), F32), biases[1]])[None]
        self.vectors = jnp.concatenate([biases[2:6], gains], 0)
        self.pieces = self.link.gather_feed(self.feed_slab)

    def attend(self, x, marks):
        self.x = x
        self.qkv, self.mix, self.lse = attention_forward(x, self.wt_qkv, self.qkv_bias, marks[0], marks[1])

    def forward(self):
        (y,) = feed(self.x, self.mix, self.wt_out, self.vectors, self.up_bias, self.pieces)
        return y

    def both(self, cot):
        (y, self.n1, self.g, self.du, self.df, self.do, self.dr1, self.dm, self.small, self.up_small) = feed(
            self.x, self.mix, self.wt_out, self.vectors, self.up_bias, self.pieces, cot
        )
        return y

    def feed_grads(self):
        n_up = self.sizes[2]
        total = self.link.reduce_feed(self.n1, self.df, self.g, self.du, n_up).astype(F32)
        return total[:n_up].T, total[n_up:]

    def backward(self, marks):
        self.dqkv, self.sums = attention_backward(self.qkv, self.dm, self.mix, self.lse, marks[2], marks[3])
        return self.dr1 + mm(self.dqkv, self.wt_qkv)

    def attention_grads(self):
        n_qkv, n_out, n_up = self.sizes
        width = self.x.shape[1]
        devices = width // n_out
        dw_qkv = mm(self.dqkv, self.x, TN).astype(BF).reshape(devices, n_qkv, width)
        dw_out = mm(self.do, self.mix, TN).astype(BF).reshape(devices, n_out, width)
        biases = jnp.stack([self.sums[0, :width], self.sums[0, 2 * width :], *(self.small[i] for i in range(4))])
        gains = self.small[4:6]
        cut = lambda rows: rows.reshape(rows.shape[0], devices, n_out).transpose(1, 0, 2).reshape(devices, -1)
        small = jnp.concatenate([cut(biases), cut(gains), self.link.up_bias_grad(self.up_small)], 1)
        small = jnp.pad(small, ((0, 0), (0, SMALL_ROWS * width - small.shape[1]))).astype(BF)
        slabs = jnp.concatenate([dw_qkv, dw_out, small.reshape(devices, SMALL_ROWS, width)], 1)
        total = self.link.reduce_attention(slabs).astype(F32)
        flat = total[n_qkv + n_out :].reshape(-1)
        return (
            total[:n_qkv].T,
            total[n_qkv : n_qkv + n_out].T,
            flat[: 6 * n_out].reshape(6, n_out),
            flat[6 * n_out : 8 * n_out].reshape(2, n_out),
            flat[8 * n_out : 8 * n_out + n_up],
        )


def body(make_link, tokens, skip_tokens, cot_first, cot_second, *rest):
    *shards, lengths, segments = rest
    link = make_link()
    length = segments.shape[1]
    place = lax.broadcasted_iota(jnp.int32, (1, length), 1)
    keys = jnp.where(place < lengths[:, None], segments, -1)
    marks = (segments.reshape(length, 1), keys, segments, keys.reshape(length, 1))
    is_first = lax.broadcasted_iota(jnp.int32, (length, 1), 0) == 0

    one, two = Block(link, shards, 0), Block(link, shards, 1)
    one.fetch()
    two.fetch()
    one.attend(tokens, marks)
    out_first = one.forward()
    two.attend(jnp.where(is_first, out_first, skip_tokens), marks)
    out_second = two.both(cot_second)
    up_two, down_two = two.feed_grads()
    d_second = two.backward(marks)
    att_two = two.attention_grads()
    grad_skip = jnp.where(is_first, 0.0, d_second)
    upstream = cot_first.astype(F32) + jnp.where(is_first, d_second, 0.0)
    one.both(upstream)
    up_one, down_one = one.feed_grads()
    grad_tokens = one.backward(marks)
    att_one = one.attention_grads()
    pair = lambda i: jnp.stack([att_one[i], att_two[i]])
    return (
        out_first, out_second, grad_tokens, grad_skip,
        pair(0), pair(1), jnp.stack([up_one, up_two]), jnp.stack([down_one, down_two]),
        pair(2), pair(3), pair(4),
    )


def solution(mesh):
    wide, narrow = mesh.shape["wide"], mesh.shape["narrow"]
    if narrow == 4 and wide % 4 == 0:
        mesh = Mesh(mesh.devices.reshape(wide // 2, 2, 2, 2), Near.axes)
        make_link, every = Near, Near.axes
    else:
        make_link, every = Far, Far.axes
    rows, last, middle = P(every, None), P(None, None, every), P(None, every, None)
    return jax.shard_map(
        functools.partial(body, make_link),
        mesh=mesh,
        in_specs=(
            rows, rows, rows, rows, last, last, last, middle, last, last, P(None, every), P(every), rows,
        ),
        out_specs=(rows, rows, rows, rows, last, last, last, middle, last, last, P(None, every)),
        check_vma=False,
    )
```

```python
import functools
import math

import jax
import jax.numpy as jnp
from jax import lax
from jax.experimental import pallas as pl
from jax.experimental.pallas import tpu as pltpu
from jax.sharding import Mesh, PartitionSpec as P

HEADS = 12
HEAD_DIM = 64
EPSILON = 1e-12
MASKED = -1e30
BF = jnp.bfloat16
F32 = jnp.float32
NT = (((1,), (1,)), ((), ()))
TN = (((0,), (0,)), ((), ()))
NN = (((1,), (0,)), ((), ()))
PARTS = 8
LANES = 128
SMALL_ROWS = 16
VMEM = pl.BlockSpec(memory_space=pltpu.VMEM)
SMEM = pl.BlockSpec(memory_space=pltpu.SMEM)


def mm(a, b, dims=NN):
    return lax.dot_general(a, b, dims, preferred_element_type=F32)


def shape(rows, cols, dtype=BF):
    return jax.ShapeDtypeStruct((rows, cols), dtype)


def call(kernel, out_shapes, scratch, *args, far=()):
    return list(pl.pallas_call(
        kernel,
        out_shape=out_shapes,
        in_specs=[SMEM if a.ndim == 1 else VMEM for a in args] + [pl.BlockSpec(memory_space=pl.ANY)] * len(far),
        out_specs=[VMEM] * len(out_shapes),
        scratch_shapes=scratch,
        compiler_params=pltpu.CompilerParams(vmem_limit_bytes=VMEM_BYTES),
    )(*args, *far))


VMEM_BYTES = 56 * 1024 * 1024


def windows(length):
    tiles = length // LANES
    return [
        (t, max(0, t - 1) * LANES, min(tiles, t + 2) * LANES) for t in range(tiles)
    ]


def far_place(at, part):
    return (at[0] ^ (part % 2)) * 4 + (at[1] ^ (part // 2 % 2)) * 2 + (at[2] ^ (part // 4))


def assemble(slabs, depth, at, pieces, wt, wt_out, small, up_bias, all_qkv, all_out, landing, sems):
    width = wt.shape[1]
    n_qkv, n_out = 3 * width // (PARTS * depth), width // (PARTS * depth)
    rest = n_qkv + n_out
    rows = landing.shape[1]
    copies, done = [], 0
    for i, piece in enumerate(pieces):
        n = piece.shape[0]
        copies.append(pltpu.make_async_copy(piece.at[:, pl.ds(0, rows), :], landing.at[pl.ds(done, n)], sems.at[i]))
        copies[-1].start()
        done += n
    small[...] = jnp.zeros_like(small)
    up_bias[...] = jnp.zeros_like(up_bias)
    done = 0
    for index, (piece, copy) in enumerate(zip(pieces, copies)):
        copy.wait()
        for i in range(piece.shape[0]):
            if slabs:
                part, first = slabs[index]
                device = (first + i) * PARTS + far_place(at, part)
            else:
                part, device = i // depth, i
            slab = landing[done].astype(F32)
            done += 1
            all_qkv[pl.ds(pl.multiple_of(device * n_qkv, 8), n_qkv), :] = slab[:n_qkv]
            all_out[pl.ds(pl.multiple_of(device * n_out, 8), n_out), :] = slab[n_qkv:rest]
            small[...] += slab[rest : rest + 8]
            line = slab[rest + 8 : rest + 9]
            if not slabs:
                shift = (i % depth - i // PARTS) * (up_bias.shape[1] // depth)
                line = pltpu.roll(line, shift % width, 1)
            up_bias[part : part + 1, :] += line[:, : up_bias.shape[1]]
    wt[...] = all_qkv[...].astype(BF)
    wt_out[...] = all_out[...].astype(BF)


def attention_forward_kernel(slabs, depth, x, seg_row, key_col, *refs):
    refs = list(refs)
    length, width = x.shape
    if slabs is None:
        wt, small, qkv, mix, lse_rows, mask = refs
    else:
        count = len(slabs) or 1
        at, pieces, refs = refs[0], refs[1 : 1 + count], refs[1 + count :]
        qkv, mix, lse_rows, wt, wt_out, small, up_bias, mask, all_qkv, all_out, landing, sems = refs
        assemble(slabs, depth, at, pieces, wt, wt_out, small, up_bias, all_qkv, all_out, landing, sems)
    for part in range(3):
        cols = slice(part * width, (part + 1) * width)
        out = mm(x[...], wt[cols, :], NT)
        if part != 1:
            out += small[part // 2 : part // 2 + 1, :]
        qkv[:, cols] = out.astype(BF)
    for t, low, high in windows(length):
        keys = lax.broadcasted_iota(jnp.int32, (high - low, LANES), 0) + low
        rows = lax.broadcasted_iota(jnp.int32, (high - low, LANES), 1) + t * LANES
        same = key_col[low:high, :] == seg_row[:, t * LANES : (t + 1) * LANES]
        mask[t, : high - low, :] = jnp.where(same | (rows == keys), 0.0, MASKED)

    def pair(p, carry):
        at_q = pl.multiple_of(p * LANES, LANES)
        at_k = pl.multiple_of(at_q + width, LANES)
        at_v = pl.multiple_of(at_q + 2 * width, LANES)
        lane = lax.broadcasted_iota(jnp.int32, (LANES, LANES), 1)
        for t, low, high in windows(length):
            here = slice(t * LANES, (t + 1) * LANES)
            q = qkv[here, pl.ds(at_q, LANES)] * HEAD_DIM ** (-0.5)
            k = qkv[low:high, pl.ds(at_k, LANES)]
            v = qkv[low:high, pl.ds(at_v, LANES)]
            outs = []
            for h in range(2):
                mine = (lane < HEAD_DIM) == (h == 0)
                s = mm(k, jnp.where(mine, q, 0).astype(BF), NT) + mask[t, : high - low, :]
                top = jnp.max(s, 0, keepdims=True)
                e = jnp.exp(s - top)
                total = jnp.sum(e, 0, keepdims=True)
                outs.append(mm((e * (1.0 / total)).astype(BF), v, TN))
                lse_rows[2 * p + h, :, here] = top + jnp.log(total)
            mix[here, pl.ds(at_q, LANES)] = jnp.where(lane < HEAD_DIM, outs[0], outs[1]).astype(BF)
        return carry

    lax.fori_loop(0, width // LANES, pair, 0)


def attention_forward(x, marks, weights, at=None, slabs=None, depth=0, rows_up=0):
    length, width = x.shape
    shapes = [shape(length, 3 * width), shape(length, width), jax.ShapeDtypeStruct((HEADS, 1, length), F32)]
    scratch = [pltpu.VMEM((length // LANES, 3 * LANES, LANES), F32)]
    args, far = list(weights), []
    if slabs is not None:
        args, far = [at], args
        shapes += [
            shape(3 * width, width), shape(width, width), shape(8, width, F32), shape(PARTS, depth * rows_up, F32),
        ]
        rows = 4 * width // (PARTS * depth) + SMALL_ROWS
        scratch += [
            pltpu.VMEM((3 * width, width), F32), pltpu.VMEM((width, width), F32),
            pltpu.VMEM((PARTS * depth, rows, width), BF), pltpu.SemaphoreType.DMA((len(far),)),
        ]
    return call(
        functools.partial(attention_forward_kernel, slabs, depth),
        shapes, scratch, x, marks[0], marks[1], *args, far=far,
    )


def attention_backward_kernel(halves, fix, clear_first, qkv, mix, lse_rows, seg_row, key_col, wt, *refs):
    refs = list(refs)
    dmix, refs = refs[:halves], refs[halves:]
    dr1, refs = refs[:halves], refs[halves:]
    if fix:
        dmix_fix, dr1_fix, *refs = refs
    dqkv, sums, dx, first, mask, dq_sum = refs
    length, width = mix.shape
    for t, low, high in windows(length):
        keys = lax.broadcasted_iota(jnp.int32, (high - low, LANES), 0) + low
        rows = lax.broadcasted_iota(jnp.int32, (high - low, LANES), 1) + t * LANES
        same = key_col[low:high, :] == seg_row[:, t * LANES : (t + 1) * LANES]
        mask[t, : high - low, :] = jnp.where(same | (rows == keys), 0.0, MASKED)

    def pair(p, carry):
        at = pl.multiple_of(p * LANES, LANES)
        at_k = pl.multiple_of(at + width, LANES)
        at_v = pl.multiple_of(at + 2 * width, LANES)
        lane = lax.broadcasted_iota(jnp.int32, (length, LANES), 1)
        q = qkv[:, pl.ds(at, LANES)] * HEAD_DIM ** (-0.5)
        dm = jnp.concatenate([half[:, pl.ds(at, LANES)] for half in dmix], 0)
        if fix:
            n = dmix_fix.shape[0]
            dm = jnp.concatenate([dm[:n] + dmix_fix[:, pl.ds(at, LANES)], dm[n:]], 0)
        product = dm.astype(F32) * mix[:, pl.ds(at, LANES)].astype(F32)
        ones_lane = lax.broadcasted_iota(jnp.int32, (8, LANES), 1)
        q_h, dm_h, lse_h, delta_h = [], [], [], []
        for h in range(2):
            mine = (lane < HEAD_DIM) == (h == 0)
            q_h.append(jnp.where(mine, q, 0).astype(BF))
            dm_h.append(jnp.where(mine, dm, 0).astype(BF))
            picks = jnp.where((ones_lane < HEAD_DIM) == (h == 0), 1.0, 0.0)
            delta_h.append(
                lax.dot_general(picks, product, NT, precision=lax.Precision.HIGHEST, preferred_element_type=F32)[:1, :]
            )
            lse_h.append(lse_rows[2 * p + h])
        dq_sum[...] = jnp.zeros_like(dq_sum)
        for t, low, high in windows(length):
            here = slice(t * LANES, (t + 1) * LANES)
            k = qkv[here, pl.ds(at_k, LANES)]
            v = qkv[here, pl.ds(at_v, LANES)]
            dk = jnp.zeros((LANES, LANES), F32)
            dv = jnp.zeros((LANES, LANES), F32)
            dq = jnp.zeros((high - low, LANES), F32)
            cover = jnp.concatenate(
                [
                    mask[r, t * LANES - low_r : (t + 1) * LANES - low_r, :]
                    for r, low_r, _ in windows(length)
                    if low <= r * LANES < high
                ],
                1,
            )
            for h in range(2):
                mine = (lane[:LANES] < HEAD_DIM) == (h == 0)
                q_one, dm_one = q_h[h][low:high], dm_h[h][low:high]
                s = mm(k, q_one, NT) + cover
                a = jnp.exp(s - lse_h[h][:, low:high])
                da = mm(v, dm_one, NT)
                ds = (a * (da - delta_h[h][:, low:high])).astype(BF)
                dv += mm(a.astype(BF), dm_one)
                dk += mm(ds, q_one)
                dq += mm(ds, jnp.where(mine, k, 0).astype(BF), TN)
            dqkv[here, pl.ds(at_k, LANES)] = dk.astype(BF)
            dqkv[here, pl.ds(at_v, LANES)] = dv.astype(BF)
            dq_sum[low:high, :] += dq
        dqkv[:, pl.ds(at, LANES)] = (dq_sum[...] * HEAD_DIM ** (-0.5)).astype(BF)
        return carry

    lax.fori_loop(0, width // LANES, pair, 0)
    sums[...] = jnp.zeros_like(sums)
    for row, part in ((0, 0), (1, 2)):
        cols = slice(part * width, (part + 1) * width)
        sums[row : row + 1, :] = mm(jnp.ones((8, length), BF), dqkv[:, cols])[:1, :]
    count = length // halves
    for i in range(halves):
        rows = slice(i * count, (i + 1) * count)
        out = mm(dqkv[rows, :], wt[...]) + dr1[i][...]
        if i == 0:
            if fix:
                n = dr1_fix.shape[0]
                out = jnp.concatenate([out[:n] + dr1_fix[...], out[n:]], 0)
            first[...] = out[: first.shape[0]]
            if clear_first:
                out = jnp.where(lax.broadcasted_iota(jnp.int32, out.shape, 0) == 0, 0.0, out)
        dx[rows, :] = out


def attention_backward(qkv, mix, lse_rows, marks, wt, dmix, dr1, fix=(), clear_first=False):
    length, width = mix.shape
    shapes = [shape(length, 3 * width), shape(8, width, F32), shape(length, width, F32), shape(16, width, F32)]
    scratch = [
        pltpu.VMEM((length // LANES, 3 * LANES, LANES), F32),
        pltpu.VMEM((length, LANES), F32),
    ]
    return call(
        functools.partial(attention_backward_kernel, len(dmix), bool(fix), clear_first),
        shapes, scratch, qkv, mix, lse_rows, marks[0], marks[1], wt, *dmix, *dr1, *fix,
    )


def attention_grads_kernel(depth, n_small, natural, at, dqkv, x, do, mix, *refs):
    refs = list(refs)
    smalls, ups, refs = refs[:n_small], refs[n_small : 2 * n_small - 1], refs[2 * n_small - 1 :]
    sent, here, by_y, by_x, both_a, both_b, all_qkv, all_out, lines = refs
    width = x.shape[1]
    n_qkv, n_out = 3 * width // (PARTS * depth), width // (PARTS * depth)
    for part in range(3):
        rows = slice(part * width, (part + 1) * width)
        all_qkv[rows, :] = mm(dqkv[:, rows], x[...], TN)
    all_out[...] = mm(do[...], mix[...], TN)
    small = sum(s[...] for s in smalls)
    up = sum(u[...] for u in ups)
    up = jnp.concatenate([up, jnp.zeros((PARTS, width - up.shape[1]), F32)], 1)
    for part in range(PARTS):
        lines[part] = up[part : part + 1]
    half = both_a.shape[0]
    for part in (4, 5, 6, 7, 3, 1, 2, 0):
        place = far_place(at, part)
        line = lax.broadcasted_iota(jnp.int32, (SMALL_ROWS - 8, width), 0) == 0
        for i in range(depth):
            device = i * PARTS + place
            tail = [small, jnp.where(line, lines[lax.div(device, depth) if natural else part], 0.0)]
            slab = jnp.concatenate(
                [
                    all_qkv[pl.ds(pl.multiple_of(device * n_qkv, 8), n_qkv), :],
                    all_out[pl.ds(pl.multiple_of(device * n_out, 8), n_out), :],
                    *tail,
                ],
                0,
            ).astype(BF)
            if part > 3:
                sent[part - 4, i] = slab
            elif part == 3:
                (both_a if i < half else both_b)[i % half] = slab
            else:
                (here, by_y, by_x)[part][i] = slab


def attention_grads(depth, at, natural, dqkv, x, do, mix, smalls, ups):
    length, width = x.shape
    rows = 4 * width // (PARTS * depth) + SMALL_ROWS
    out = lambda *lead: jax.ShapeDtypeStruct((*lead, rows, width), BF)
    shapes = [out(4, depth), out(depth), out(depth), out(depth), out(depth // 2), out(depth // 2)]
    scratch = [
        pltpu.VMEM((3 * width, width), F32), pltpu.VMEM((width, width), F32), pltpu.VMEM((PARTS, 1, width), F32),
    ]
    return call(
        functools.partial(attention_grads_kernel, depth, len(smalls), natural),
        shapes, scratch, at, dqkv, x, do, mix, *smalls, *ups,
    )


def norm(values):
    centred = values - jnp.mean(values, -1, keepdims=True)
    inverse = lax.rsqrt(jnp.mean(centred * centred, -1, keepdims=True) + EPSILON)
    return centred * inverse, inverse


def norm_back(upstream, scaled, inverse, gain):
    through = upstream * gain
    return inverse * (
        through
        - jnp.mean(through, -1, keepdims=True)
        - scaled * jnp.mean(through * scaled, -1, keepdims=True)
    )


def normal_terms(u):
    size = jnp.abs(u) * (1.0 / math.sqrt(2.0))
    bell = jnp.exp(-(size * size))
    s = 1.0 / (1.0 + 0.3275911 * size)
    tail = s * (0.5 * 0.254829592 + s * (0.5 * -0.284496736 + s * (0.5 * 1.421413741 + s * (0.5 * -1.453152027 + s * (0.5 * 1.061405429)))))
    tail = tail * bell
    return jnp.where(u > 0, 1.0 - tail, tail), bell * (1.0 / math.sqrt(2.0 * math.pi))


def feed_kernel(pieces_at, skip_rows, start, clear_first, backward, *refs):
    refs = list(refs)
    take = lambda n: [refs.pop(0) for _ in range(n)]
    x, mix, w_out, vectors, up_bias = take(5)
    (cot,) = take(1) if backward else (None,)
    pieces = take(len(pieces_at))
    if backward:
        y, n1_out, g_out, du_out, df_out, do_out, dr1_out, dm_out, small, up_small, slabs, sems, slope = refs
        small[...] = jnp.zeros_like(small)
        up_small[...] = jnp.zeros_like(up_small)
    else:
        y, slabs, sems = refs
    count, width = y.shape
    half = slabs.shape[1] // 2
    each = slabs.shape[0] // PARTS
    copies = []
    for i, (piece, at) in enumerate(zip(pieces, pieces_at)):
        n = piece.shape[0]
        copies.append(
            pltpu.make_async_copy(piece.at[:, pl.ds(skip_rows, 2 * half), :], slabs.at[pl.ds(at, n)], sems.at[i])
        )
        copies[-1].start()

    def weights(part, lower):
        for copy, at in zip(list(copies), pieces_at):
            if copy is not None and at < (part + 1) * each:
                copy.wait()
                copies[copies.index(copy)] = None
        top = half if lower else 0
        return slabs[part * each : (part + 1) * each, top : top + half, :].reshape(each * half, width)

    b_out, b_down, shift_one, shift_two, gain_one, gain_two = (vectors[i : i + 1, :] for i in range(2, 8))
    here = slice(start, start + count)
    r1 = x[here, :].astype(F32) + mm(mix[here, :], w_out[...], NT) + b_out
    z1, q1 = norm(r1)
    n1 = (z1 * gain_one + shift_one).astype(BF)
    acc = n1.astype(F32) + b_down
    for part in range(PARTS):
        u = mm(n1, weights(part, False), NT) + up_bias[part : part + 1, :]
        size = u.shape[1]
        cols = slice(part * size, (part + 1) * size)
        big, bell = normal_terms(u)
        g = (u * big).astype(BF)
        if backward:
            g_out[:, cols] = g
            slope[:, cols] = big + u * bell
        acc += mm(g, weights(part, True))
    z2, q2 = norm(acc)
    y[...] = (z2 * gain_two + shift_two).astype(BF)
    if backward:
        e = cot[here, :].astype(F32)
        if clear_first:
            e = jnp.where(lax.broadcasted_iota(jnp.int32, e.shape, 0) + start == 0, 0.0, e)
        small[5:6, :] += jnp.sum(e, 0, keepdims=True)
        small[7:8, :] += jnp.sum(e * z2, 0, keepdims=True)
        dr2 = norm_back(e, z2, q2, gain_two)
        df = dr2.astype(BF)
        small[3:4, :] += jnp.sum(df.astype(F32), 0, keepdims=True)
        dn1 = dr2
        for part in range(PARTS):
            da = mm(df, weights(part, True), NT)
            size = da.shape[1]
            cols = slice(part * size, (part + 1) * size)
            du = (da * slope[:, cols]).astype(BF)
            du_out[:, cols] = du
            up_small[part : part + 1, :] += jnp.sum(du.astype(F32), 0, keepdims=True)
            dn1 += mm(du, weights(part, False))
        small[4:5, :] += jnp.sum(dn1, 0, keepdims=True)
        small[6:7, :] += jnp.sum(dn1 * z1, 0, keepdims=True)
        dr1 = norm_back(dn1, z1, q1, gain_one)
        do = dr1.astype(BF)
        small[2:3, :] += jnp.sum(do.astype(F32), 0, keepdims=True)
        dm_out[...] = mm(do, w_out[...]).astype(BF)
        n1_out[...] = n1
        df_out[...] = df
        do_out[...] = do
        dr1_out[...] = dr1


def feed(x, mix, w_out, vectors, up_bias, pieces, pieces_at, cot=None, start=0, count=None, clear_first=False, skip_rows=0):
    width = x.shape[1]
    count = count or x.shape[0]
    hidden = PARTS * up_bias.shape[1]
    wide, high = shape(count, width), shape(count, hidden)
    rows = pieces[0].shape[1] - skip_rows
    shapes = [wide]
    scratch = [pltpu.VMEM((2 * hidden // rows, rows, width), BF), pltpu.SemaphoreType.DMA((len(pieces),))]
    args = [x, mix, w_out, vectors, up_bias]
    if cot is not None:
        args.append(cot)
        shapes += [wide, high, high, wide, wide, shape(count, width, F32), wide, shape(8, width, F32), shape(*up_bias.shape, F32)]
        scratch.append(pltpu.VMEM((count, hidden), F32))
    return call(
        functools.partial(feed_kernel, pieces_at, skip_rows, start, clear_first, cot is not None),
        shapes, scratch, *args, far=pieces,
    )


def feed_grads_kernel(first, layout, halves, received, *refs):
    refs = list(refs)
    n1, df, g, du = (refs[i * halves : (i + 1) * halves] for i in range(4))
    refs = refs[4 * halves :]
    got = [refs.pop(0) for _ in range(received)]
    stacked = layout is None
    for index in range(refs[0].shape[0] if stacked else len(layout)):
        part = first + index
        outs = [refs[0].at[index]] if stacked else [refs.pop(0) for _ in range(layout[index])]
        size = g[0].shape[1] // PARTS
        cols = slice(part * size, (part + 1) * size)
        for lower, (left, right) in enumerate(((du, n1), (g, df))):
            full = sum(mm(a[:, cols], b[...], TN) for a, b in zip(left, right))
            at = 0
            for out in outs:
                slabs, half = out.shape[0], out.shape[1] // 2
                rows = slice(lower * half, (lower + 1) * half)
                value = full[at * half : (at + slabs) * half].reshape(slabs, half, out.shape[2])
                if received:
                    value += got[0][index, at : at + slabs, rows, :].astype(F32)
                out[:, rows, :] = value.astype(BF)
                at += slabs


def feed_grads(first, shapes, layout, n1, df, g, du, *received):
    width = n1[0].shape[1]
    outs = [jax.ShapeDtypeStruct((*lead, width), BF) for lead in shapes]
    return call(
        functools.partial(feed_grads_kernel, first, layout, len(n1), len(received)),
        outs, [], *n1, *df, *g, *du, *received,
    )


def feed_grads_all(halves_n, depth, half, n1, df, g, du, store):
    for part in range(PARTS):
        size = g[0].shape[1] // PARTS
        cols = slice(part * size, (part + 1) * size)
        for lower, (left, right) in enumerate(((du, n1), (g, df))):
            full = sum(mm(a[:, cols], b[...], TN) for a, b in zip(left, right)).astype(BF)
            store(part, lower, full.reshape(depth, half, -1))


def feed_grads_spread_kernel(depth, halves, at, *refs):
    refs = list(refs)
    n1, df, g, du = (refs[i * halves : (i + 1) * halves] for i in range(4))
    sent, here, by_y, by_x, both_a, both_b, all_rows = refs[4 * halves :]
    half = all_rows.shape[1] // 2

    def store(part, lower, value):
        all_rows[part * depth : (part + 1) * depth, lower * half : (lower + 1) * half, :] = value

    feed_grads_all(halves, depth, half, n1, df, g, du, store)
    split = both_a.shape[0]
    for part in (4, 5, 6, 7, 3, 1, 2, 0):
        place = far_place(at, part)
        for i in range(depth):
            slab = all_rows[i * PARTS + place]
            if part > 3:
                sent[part - 4, i] = slab
            elif part == 3:
                (both_a if i < split else both_b)[i % split] = slab
            else:
                (here, by_y, by_x)[part][i] = slab


def feed_grads_order_kernel(depth, halves, at, *refs):
    refs = list(refs)
    n1, df, g, du = (refs[i * halves : (i + 1) * halves] for i in range(4))
    (out,) = refs[4 * halves :]
    half = out.shape[1] // 2

    def store(part, lower, value):
        place = far_place(at, part)
        for i in range(depth):
            out[i * PARTS + place, lower * half : (lower + 1) * half, :] = value[i]

    feed_grads_all(halves, depth, half, n1, df, g, du, store)


def feed_grads_natural(spread, depth, half, at, n1, df, g, du):
    width = n1[0].shape[1]
    out = lambda *lead: jax.ShapeDtypeStruct((*lead, 2 * half, width), BF)
    if spread:
        shapes = [out(4, depth), out(depth), out(depth), out(depth), out(depth // 2), out(depth // 2)]
        scratch = [pltpu.VMEM((PARTS * depth, 2 * half, width), BF)]
    else:
        shapes, scratch = [out(PARTS * depth)], []
    kernel = feed_grads_spread_kernel if spread else feed_grads_order_kernel
    return call(functools.partial(kernel, depth, len(n1)), shapes, scratch, at, *n1, *df, *g, *du)


def after(values, *before):
    return lax.optimization_barrier((values, before))[0]


def swap(array, axis):
    return lax.ppermute(array, axis, [(0, 1), (1, 0)])


def swaps(arrays, axis):
    return [swap(a, axis) for a in arrays]


def marks_of(lengths, segments):
    length = segments.shape[1]
    place = lax.broadcasted_iota(jnp.int32, (1, length), 1)
    keys = jnp.where(place < lengths[:, None], segments, -1)
    return segments, keys.reshape(length, 1)


class Near:
    axes = ("z", "y", "x", "core")

    def __init__(self, shards):
        self.shards = shards
        self.depth = lax.axis_size("z")
        y, x, core = (lax.axis_index(name) for name in self.axes[1:])
        self.at = jnp.stack([y, x, core])
        self.z = lax.axis_index("z")
        self.device = self.z * PARTS + y * 4 + x * 2 + core
        w_qkv, w_out, w_up = shards[:3]
        self.n_qkv, self.n_out, self.n_up = w_qkv.shape[2], w_out.shape[2], w_up.shape[2]
        half = self.depth // 2
        own = [(0, 0), (1, 0), (2, 0), (3, 0), (3, half)]
        self.slabs = own + [(part + 4, first) for part, first in own]

    def slab_pair(self, index):
        w_qkv, w_out, w_up, w_down, biases, gains, up_bias = (s[index] for s in self.shards)
        width = w_qkv.shape[0]
        natural = lax.dynamic_update_slice(
            jnp.zeros((8, width), BF), jnp.concatenate([biases, gains], 0), (0, self.device * self.n_out)
        )
        line = lax.dynamic_update_slice(jnp.zeros((8, width), BF), up_bias[None], (0, self.z * self.n_up))
        attention = jnp.concatenate([w_qkv.T, w_out.T, natural, line], 0)
        return attention, jnp.concatenate([w_up.T, w_down], 0)

    def along_z(self, slab):
        return lax.all_gather(slab, "z", axis=0, tiled=False)

    def near(self, here):
        return [here, swap(here, "y"), swap(here, "x")]

    def diagonal(self, near):
        half = self.depth // 2
        return [swap(near[1][:half], "x"), swap(near[2][half:], "y")]

    def attend(self, x, marks, pieces):
        slabs = self.slabs if len(pieces) > 1 else []
        out = attention_forward(x, marks, pieces, self.at, slabs, self.depth, self.n_up)
        return dict(zip(("x", "qkv", "mix", "lse", "wt", "wt_out", "small", "up_bias"), [x, *out]))

    def feed(self, kept, pieces, cot, start, count, clear_first=False):
        pieces_at = [part * self.depth + first for part, first in self.slabs][: len(pieces)]
        out = feed(
            kept["x"], kept["mix"], kept["wt_out"], kept["small"], kept["up_bias"], pieces, pieces_at,
            cot, start, count, clear_first, pieces[0].shape[1] - 2 * self.n_up,
        )
        return dict(zip(("y", "n1", "g", "du", "df", "do", "dr1", "dm", "small", "up"), out))

    def feed_sent(self, halves):
        lists = [[h[name] for h in halves] for name in ("n1", "df", "g", "du")]
        (sent,) = feed_grads(4, [(4, self.depth, 2 * self.n_up)], None, *lists)
        return sent

    def feed_kept(self, halves, received):
        lists = [[h[name] for h in halves] for name in ("n1", "df", "g", "du")]
        full, half = (self.depth, 2 * self.n_up), (self.depth // 2, 2 * self.n_up)
        return feed_grads(0, [full, full, full, half, half], [1, 1, 1, 2], *lists, received)

    def feed_natural(self, halves, spread):
        lists = [[h[name] for h in halves] for name in ("n1", "df", "g", "du")]
        return feed_grads_natural(spread, self.depth, self.n_up, self.at, *lists)

    def reduce_diagonal(self, both):
        return [swap(both[0], "x"), swap(both[1], "y")]

    def add_diagonal(self, by_y, by_x, got):
        half = self.depth // 2
        return [by_y.at[:half].add(got[0]), by_x.at[half:].add(got[1])]

    def reduce_near(self, added):
        return [swap(added[0], "y"), swap(added[1], "x")]

    def reduce_z(self, here, got):
        return lax.psum_scatter(here + got[0] + got[1], "z", scatter_dimension=0, tiled=False)

    def attention_grads(self, kept, dqkv, do, smalls, ups, natural):
        sent, here, by_y, by_x, both_a, both_b = attention_grads(
            self.depth, self.at, natural, dqkv, kept["x"], do, kept["mix"], smalls, ups
        )
        return sent, [here, by_y, by_x, both_a, both_b]

    def add_received(self, kept, received):
        half = self.depth // 2
        here, by_y, by_x, both_a, both_b = kept
        return [
            here + received[0], by_y + received[1], by_x + received[2],
            both_a + received[3, :half], both_b + received[3, half:],
        ]

    def attention_outs(self, total, natural):
        total = total.astype(F32)
        n_qkv, n_out, n_up = self.n_qkv, self.n_out, self.n_up
        small = total[n_qkv + n_out :]
        own = lax.dynamic_slice(small, (0, self.device * n_out), (8, n_out))
        up = lax.dynamic_slice(small, (8, (self.device % self.depth if natural else self.z) * n_up), (1, n_up))[0]
        return total[:n_qkv].T, total[n_qkv : n_qkv + n_out].T, own[:6], own[6:], up

    def first_row_terms(self, fix):
        width = fix["n1"].shape[1]
        rows = jnp.stack([fix["n1"][0], fix["df"][0]]).reshape(1, 2 * width)
        table = jnp.stack([fix["du"][0].reshape(PARTS, self.depth, self.n_up), fix["g"][0].reshape(PARTS, self.depth, self.n_up)], 2)
        table = table.reshape(1, PARTS, -1)
        for axis in ("core", "x", "y"):
            n, far = table.shape[0], table.shape[1] // 2
            flat = jnp.concatenate([rows, table[:, far:].reshape(n, -1)], 1)
            got = swap(flat, axis)
            rows = jnp.concatenate([rows, got[:, : 2 * width]], 0)
            table = jnp.concatenate([table[:, :far], got[:, 2 * width :].reshape(n, far, -1)], 0)
        n = rows.shape[0]
        flat = jnp.concatenate([rows, table.reshape(n, -1)], 1)
        step = 1
        while step < self.depth:
            pairs = [(i, i ^ step) for i in range(self.depth)]
            flat = jnp.concatenate([flat, lax.ppermute(flat, "z", pairs)], 0)
            step *= 2
        own = flat[:, 2 * width :].reshape(flat.shape[0], self.depth, 2, self.n_up)
        own = lax.dynamic_index_in_dim(own, self.z, 1, keepdims=False)
        up = mm(own[:, 0], flat[:, :width], TN)
        down = mm(own[:, 1], flat[:, width : 2 * width], TN)
        return up, down


def near_body(tokens, skip_tokens, cot_first, cot_second, *rest):
    *shards, lengths, segments = rest
    link = Near(shards)
    marks = marks_of(lengths, segments)
    length = segments.shape[1]
    half = length // 2
    is_first = lax.broadcasted_iota(jnp.int32, (length, 1), 0) == 0

    slab_a1, slab_m1 = link.slab_pair(0)
    a1 = link.along_z(slab_a1)
    m1 = link.along_z(slab_m1)
    b2 = [lax.all_gather(after(jnp.concatenate(link.slab_pair(1), 0), a1), link.axes, axis=0, tiled=False)]
    a1 = link.near(a1)
    a1 += link.diagonal(a1)
    m1 = link.near(after(m1, a1))
    a1 += swaps(a1, "core")
    one = link.attend(*after((tokens, marks, a1), m1[0]))
    m1 = after(m1, one["mix"])
    m1 += link.diagonal(m1)
    m1 += swaps(m1, "core")
    one_a = link.feed(one, m1, cot_first, 0, half, True)
    one_b = link.feed(*after((one, m1, cot_first), one_a["y"]), half, half)
    (all_m1,) = link.feed_natural([one_a, one_b], False)
    sum_m1 = lax.psum_scatter(all_m1, link.axes, scatter_dimension=0, tiled=False).astype(F32)
    out_first = jnp.concatenate([one_a["y"], one_b["y"]], 0)
    second_in = jnp.where(is_first, out_first, skip_tokens)
    two = link.attend(*after((second_in, marks), all_m1), b2)
    two_a = link.feed(*after((two, b2, cot_second), two["mix"]), 0, half)
    two_b = link.feed(*after((two, b2, cot_second), two_a["y"]), half, half)
    sent_m2, *kept_m2 = link.feed_natural([two_a, two_b], True)
    dqkv2, sums2, grad_skip, first2 = attention_backward(
        two["qkv"], two["mix"], two["lse"], marks, two["wt"],
        *after(([two_a["dm"], two_b["dm"]], [two_a["dr1"], two_b["dr1"]]), kept_m2), clear_first=True,
    )
    kept_m2 = link.add_received(*after((kept_m2, swap(sent_m2, "core")), dqkv2))
    got_m2 = link.reduce_diagonal(kept_m2[3:])
    upstream = jnp.where(is_first[:16], cot_first[:16].astype(F32) + first2, 0.0)
    fix = link.feed(one, m1, after(upstream, kept_m2), 0, 16)
    added_m2 = link.add_diagonal(*after((kept_m2[1], kept_m2[2], got_m2), fix["y"]))
    got_m2 = link.reduce_near(added_m2)
    dqkv1, sums1, grad_tokens, _ = attention_backward(
        one["qkv"], one["mix"], one["lse"], marks, one["wt"],
        *after(([one_a["dm"], one_b["dm"]], [one_a["dr1"], one_b["dr1"]]), added_m2), fix=(fix["dm"], fix["dr1"]),
    )
    fix, one_a, one_b, two_a, two_b = after((fix, one_a, one_b, two_a, two_b), dqkv1)
    do1 = jnp.concatenate([one_a["do"], one_b["do"]], 0).at[:16].add(fix["do"])
    sent_a1, kept_a1 = link.attention_grads(
        one, dqkv1, do1,
        [sums1, one_a["small"], one_b["small"], fix["small"]], [one_a["up"], one_b["up"], fix["up"]], False,
    )
    sent_a2, kept_a2 = link.attention_grads(
        two, after(dqkv2, got_m2, sent_a1), jnp.concatenate([two_a["do"], two_b["do"]], 0),
        [sums2, two_a["small"], two_b["small"]], [two_a["up"], two_b["up"]], True,
    )
    sum_m2 = link.reduce_z(kept_m2[0], got_m2).astype(F32)
    kept_a1 = link.add_received(*after((kept_a1, swap(sent_a1, "core")), sent_a2))
    got_a1 = link.reduce_diagonal(kept_a1[3:])
    kept_a2 = link.add_received(*after((kept_a2, swap(sent_a2, "core")), kept_a1))
    got_a2 = link.reduce_diagonal(kept_a2[3:])
    got_a1 = link.reduce_near(link.add_diagonal(*after(kept_a1[1:3] + [got_a1], kept_a2)))
    got_a2 = link.reduce_near(link.add_diagonal(*kept_a2[1:3], got_a2))
    sum_a1 = link.reduce_z(after(kept_a1[0], sum_m2), got_a1)
    sum_a2 = link.reduce_z(after(kept_a2[0], sum_a1.astype(F32)), got_a2)

    n_up = link.n_up
    up_fix, down_fix = link.first_row_terms(fix)
    outs = [link.attention_outs(sum_a1, False), link.attention_outs(sum_a2, True)]
    pair = lambda i: jnp.stack([outs[0][i], outs[1][i]])
    return (
        out_first, jnp.concatenate([two_a["y"], two_b["y"]], 0), grad_tokens, grad_skip,
        pair(0), pair(1),
        jnp.stack([(sum_m1[:n_up] + up_fix).T, sum_m2[:n_up].T]),
        jnp.stack([sum_m1[n_up:] + down_fix, sum_m2[n_up:]]),
        pair(2), pair(3), pair(4),
    )


def far_body(tokens, skip_tokens, cot_first, cot_second, *rest):
    *shards, lengths, segments = rest
    axes = ("wide", "narrow")
    devices = lax.axis_size("wide") * lax.axis_size("narrow")
    marks = marks_of(lengths, segments)
    length, width = tokens.shape
    is_first = lax.broadcasted_iota(jnp.int32, (length, 1), 0) == 0
    gather = lambda a: lax.all_gather(a, axes, axis=0, tiled=True)
    scatter = lambda a: lax.psum_scatter(a, axes, scatter_dimension=0, tiled=True)

    def fetch(index):
        w_qkv, w_out, w_up, w_down, biases, gains, up_bias = (s[index] for s in shards)
        small = gather(jnp.concatenate([biases, gains], 0).T).T.astype(F32)
        up, down = (gather(w).reshape(PARTS, -1, width) for w in (w_up.T, w_down))
        both = jnp.concatenate([up, down], 1)
        return (
            gather(w_qkv.T), gather(w_out.T), small, gather(up_bias).astype(F32).reshape(PARTS, -1),
            [both],
        )

    def forward(x, weights):
        wt, wt_out, small, up_bias, pieces = weights
        qkv, mix, lse = attention_forward(x, marks, (wt, small))
        return (qkv, mix, lse), feed(x, mix, wt_out, small, up_bias, pieces, [0])[0]

    def backward(x, weights, kept, cot, clear_first):
        wt, wt_out, small, up_bias, pieces = weights
        qkv, mix, lse = kept
        y, n1, g, du, df, do, dr1, dm, sums, up_sums = feed(x, mix, wt_out, small, up_bias, pieces, [0], cot)
        dqkv, more, dx, first = attention_backward(qkv, mix, lse, marks, wt, [dm], [dr1], clear_first=clear_first)
        rows = 2 * up_bias.shape[1]
        lists = [[n1], [df], [g], [du]]
        parts = jnp.concatenate([feed_grads(i, [(4, 1, rows)], None, *lists)[0][:, 0] for i in (0, 4)], 0)
        up, down = (p.reshape(-1, width) for p in (parts[:, : rows // 2], parts[:, rows // 2 :]))
        sums = scatter((sums + more).T).T
        grads = (
            scatter(mm(dqkv, x, TN).astype(BF)).astype(F32).T,
            scatter(mm(do, mix, TN).astype(BF)).astype(F32).T,
            scatter(up).astype(F32).T,
            scatter(down).astype(F32),
            sums[:6], sums[6:], scatter(up_sums.reshape(-1)),
        )
        return y, dx, first, grads

    one, two = fetch(0), fetch(1)
    kept_one, out_first = forward(tokens, one)
    second_in = jnp.where(is_first, out_first, skip_tokens)
    kept_two, _ = forward(second_in, two)
    out_second, grad_skip, first, grads_two = backward(second_in, two, kept_two, cot_second, True)
    first = jnp.concatenate([first, jnp.zeros((length - first.shape[0], width), F32)], 0)
    upstream = cot_first.astype(F32) + jnp.where(is_first, first, 0.0)
    _, grad_tokens, _, grads_one = backward(tokens, one, kept_one, upstream, False)
    return (out_first, out_second, grad_tokens, grad_skip, *(jnp.stack(p) for p in zip(grads_one, grads_two)))


def solution(mesh):
    wide, narrow = mesh.shape["wide"], mesh.shape["narrow"]
    if narrow == 4 and wide % 4 == 0:
        mesh = Mesh(mesh.devices.reshape(wide // 2, 2, 2, 2), Near.axes)
        body, every = near_body, Near.axes
    else:
        body, every = far_body, ("wide", "narrow")
    rows, last, middle = P(every, None), P(None, None, every), P(None, every, None)
    return jax.shard_map(
        body,
        mesh=mesh,
        in_specs=(
            rows, rows, rows, rows, last, last, last, middle, last, last, P(None, every), P(every), rows,
        ),
        out_specs=(rows, rows, rows, rows, last, last, last, middle, last, last, P(None, every)),
        check_vma=False,
    )
```

```python
import functools
import math

import jax
import jax.numpy as jnp
from jax import lax
from jax.experimental import pallas as pl
from jax.experimental.pallas import tpu as pltpu
from jax.sharding import Mesh, PartitionSpec as P

HEADS = 12
HEAD_DIM = 64
EPSILON = 1e-12
MASKED = -1e30
BF = jnp.bfloat16
F32 = jnp.float32
NT = (((1,), (1,)), ((), ()))
TN = (((0,), (0,)), ((), ()))
NN = (((1,), (0,)), ((), ()))
PARTS = 8
LANES = 128
SMALL_ROWS = 16
VMEM = pl.BlockSpec(memory_space=pltpu.VMEM)
SMEM = pl.BlockSpec(memory_space=pltpu.SMEM)


def mm(a, b, dims=NN):
    return lax.dot_general(a, b, dims, preferred_element_type=F32)


def shape(rows, cols, dtype=BF):
    return jax.ShapeDtypeStruct((rows, cols), dtype)


def call(kernel, out_shapes, scratch, work, *args, far=(), far_outs=0, wait=()):
    before, ahead = len(args) + len(far), len(wait)
    inner = kernel
    kernel = lambda *refs: inner(*refs[:before], *refs[before + ahead :])
    return list(pl.pallas_call(
        kernel,
        out_shape=out_shapes,
        in_specs=[SMEM if a.ndim == 1 else VMEM for a in args] + [pl.BlockSpec(memory_space=pl.ANY)] * (len(far) + ahead),
        out_specs=[VMEM] * (len(out_shapes) - far_outs) + [pl.BlockSpec(memory_space=pl.ANY)] * far_outs,
        scratch_shapes=scratch,
        compiler_params=pltpu.CompilerParams(vmem_limit_bytes=VMEM_BYTES),
        cost_estimate=pl.CostEstimate(flops=int(work * 1.15e9), bytes_accessed=0, transcendentals=0),
    )(*args, *far, *wait))


VMEM_BYTES = 56 * 1024 * 1024


def windows(length):
    tiles = length // LANES
    return [
        (t, max(0, t - 1) * LANES, min(tiles, t + 2) * LANES) for t in range(tiles)
    ]


def far_place(at, part):
    return (at[0] ^ (part % 2)) * 4 + (at[1] ^ (part // 2 % 2)) * 2 + (at[2] ^ (part // 4))


def assemble(slabs, depth, at, pieces, wt, wt_out, small, up_bias, all_qkv, all_out, landing, sems):
    width = wt.shape[1]
    n_qkv, n_out = 3 * width // (PARTS * depth), width // (PARTS * depth)
    rest = n_qkv + n_out
    rows = landing.shape[1]
    copies, done = [], 0
    for i, piece in enumerate(pieces):
        n = piece.shape[0]
        copies.append(pltpu.make_async_copy(piece.at[:, pl.ds(0, rows), :], landing.at[pl.ds(done, n)], sems.at[i]))
        copies[-1].start()
        done += n
    small[...] = jnp.zeros_like(small)
    up_bias[...] = jnp.zeros_like(up_bias)
    done = 0
    for index, (piece, copy) in enumerate(zip(pieces, copies)):
        copy.wait()
        for i in range(piece.shape[0]):
            if slabs:
                part, first = slabs[index]
                device = (first + i) * PARTS + far_place(at, part)
            else:
                part, device = i // depth, i
            slab = landing[done].astype(F32)
            done += 1
            all_qkv[pl.ds(pl.multiple_of(device * n_qkv, 8), n_qkv), :] = slab[:n_qkv]
            all_out[pl.ds(pl.multiple_of(device * n_out, 8), n_out), :] = slab[n_qkv:rest]
            small[...] += slab[rest : rest + 8]
            line = slab[rest + 8 : rest + 9]
            if not slabs:
                shift = (i % depth - i // PARTS) * (up_bias.shape[1] // depth)
                line = pltpu.roll(line, shift % width, 1)
            up_bias[part : part + 1, :] += line[:, : up_bias.shape[1]]
    wt[...] = all_qkv[...].astype(BF)
    wt_out[...] = all_out[...].astype(BF)


def attention_forward_kernel(slabs, depth, x, seg_row, key_col, *refs):
    refs = list(refs)
    length, width = x.shape
    if slabs is None:
        wt, small, qkv, mix, lse_rows, mask = refs
    else:
        count = len(slabs) or 1
        at, pieces, refs = refs[0], refs[1 : 1 + count], refs[1 + count :]
        qkv, mix, lse_rows, wt, wt_out, small, up_bias, mask, all_qkv, all_out, landing, sems = refs
        assemble(slabs, depth, at, pieces, wt, wt_out, small, up_bias, all_qkv, all_out, landing, sems)
    for part in range(3):
        cols = slice(part * width, (part + 1) * width)
        out = mm(x[...], wt[cols, :], NT)
        if part != 1:
            out += small[part // 2 : part // 2 + 1, :]
        qkv[:, cols] = out.astype(BF)
    for t, low, high in windows(length):
        keys = lax.broadcasted_iota(jnp.int32, (high - low, LANES), 0) + low
        rows = lax.broadcasted_iota(jnp.int32, (high - low, LANES), 1) + t * LANES
        same = key_col[low:high, :] == seg_row[:, t * LANES : (t + 1) * LANES]
        mask[t, : high - low, :] = jnp.where(same | (rows == keys), 0.0, MASKED)

    def pair(p, carry):
        at_q = pl.multiple_of(p * LANES, LANES)
        at_k = pl.multiple_of(at_q + width, LANES)
        at_v = pl.multiple_of(at_q + 2 * width, LANES)
        lane = lax.broadcasted_iota(jnp.int32, (LANES, LANES), 1)
        for t, low, high in windows(length):
            here = slice(t * LANES, (t + 1) * LANES)
            q = qkv[here, pl.ds(at_q, LANES)] * HEAD_DIM ** (-0.5)
            k = qkv[low:high, pl.ds(at_k, LANES)]
            v = qkv[low:high, pl.ds(at_v, LANES)]
            outs = []
            for h in range(2):
                mine = (lane < HEAD_DIM) == (h == 0)
                s = mm(k, jnp.where(mine, q, 0).astype(BF), NT) + mask[t, : high - low, :]
                top = jnp.max(s, 0, keepdims=True)
                e = jnp.exp(s - top)
                total = jnp.sum(e, 0, keepdims=True)
                outs.append(mm((e * (1.0 / total)).astype(BF), v, TN))
                lse_rows[2 * p + h, :, here] = top + jnp.log(total)
            mix[here, pl.ds(at_q, LANES)] = jnp.where(lane < HEAD_DIM, outs[0], outs[1]).astype(BF)
        return carry

    lax.fori_loop(0, width // LANES, pair, 0)


def attention_forward(x, marks, weights, at=None, slabs=None, depth=0, rows_up=0):
    length, width = x.shape
    shapes = [shape(length, 3 * width), shape(length, width), jax.ShapeDtypeStruct((HEADS, 1, length), F32)]
    scratch = [pltpu.VMEM((length // LANES, 3 * LANES, LANES), F32)]
    args, far = list(weights), []
    if slabs is not None:
        args, far = [at], args
        shapes += [
            shape(3 * width, width), shape(width, width), shape(8, width, F32), shape(PARTS, depth * rows_up, F32),
        ]
        rows = 4 * width // (PARTS * depth) + SMALL_ROWS
        scratch += [
            pltpu.VMEM((3 * width, width), F32), pltpu.VMEM((width, width), F32),
            pltpu.VMEM((PARTS * depth, rows, width), BF), pltpu.SemaphoreType.DMA((len(far),)),
        ]
    return call(
        functools.partial(attention_forward_kernel, slabs, depth),
        shapes, scratch, 15, x, marks[0], marks[1], *args, far=far,
    )


def attention_backward_kernel(fix, clear_first, depth, natural, n_small, *refs):
    refs = list(refs)
    take = lambda n: [refs.pop(0) for _ in range(n)]
    grads = depth > 0
    (at,) = take(1) if grads else (None,)
    qkv, mix, lse_rows, seg_row, key_col, dmix = take(6)
    dmix_fix, dr1_fix = take(2) if fix else (None, None)
    (do_fix,) = take(1) if fix and grads else (None,)
    smalls, ups = take(n_small), take(n_small)
    far = take(4 if grads else 2)
    if grads:
        dx, first, sent, kept, mask, dq_sum, dqkv, all_qkv, all_out, lines, *near, sems = refs
        wt, dr1, x, do = near
    else:
        dqkv, sums, dx, first, mask, dq_sum, *near, sems = refs
        wt, dr1 = near
    copies = [pltpu.make_async_copy(a, b, sems.at[i]) for i, (a, b) in enumerate(zip(far, near))]
    for copy in copies:
        copy.start()
    length, width = mix.shape
    for t, low, high in windows(length):
        keys = lax.broadcasted_iota(jnp.int32, (high - low, LANES), 0) + low
        rows = lax.broadcasted_iota(jnp.int32, (high - low, LANES), 1) + t * LANES
        same = key_col[low:high, :] == seg_row[:, t * LANES : (t + 1) * LANES]
        mask[t, : high - low, :] = jnp.where(same | (rows == keys), 0.0, MASKED)

    def pair(p, carry):
        at_q = pl.multiple_of(p * LANES, LANES)
        at_k = pl.multiple_of(at_q + width, LANES)
        at_v = pl.multiple_of(at_q + 2 * width, LANES)
        lane = lax.broadcasted_iota(jnp.int32, (length, LANES), 1)
        q = qkv[:, pl.ds(at_q, LANES)] * HEAD_DIM ** (-0.5)
        dm = dmix[:, pl.ds(at_q, LANES)]
        if fix:
            n = dmix_fix.shape[0]
            dm = jnp.concatenate([dm[:n] + dmix_fix[:, pl.ds(at_q, LANES)], dm[n:]], 0)
        product = dm.astype(F32) * mix[:, pl.ds(at_q, LANES)].astype(F32)
        ones_lane = lax.broadcasted_iota(jnp.int32, (8, LANES), 1)
        q_h, dm_h, lse_h, delta_h = [], [], [], []
        for h in range(2):
            mine = (lane < HEAD_DIM) == (h == 0)
            q_h.append(jnp.where(mine, q, 0).astype(BF))
            dm_h.append(jnp.where(mine, dm, 0).astype(BF))
            picks = jnp.where((ones_lane < HEAD_DIM) == (h == 0), 1.0, 0.0)
            delta_h.append(
                lax.dot_general(picks, product, NT, precision=lax.Precision.HIGHEST, preferred_element_type=F32)[:1, :]
            )
            lse_h.append(lse_rows[2 * p + h])
        dq_sum[...] = jnp.zeros_like(dq_sum)
        for t, low, high in windows(length):
            here = slice(t * LANES, (t + 1) * LANES)
            k = qkv[here, pl.ds(at_k, LANES)]
            v = qkv[here, pl.ds(at_v, LANES)]
            dk = jnp.zeros((LANES, LANES), F32)
            dv = jnp.zeros((LANES, LANES), F32)
            dq = jnp.zeros((high - low, LANES), F32)
            cover = jnp.concatenate(
                [
                    mask[r, t * LANES - low_r : (t + 1) * LANES - low_r, :]
                    for r, low_r, _ in windows(length)
                    if low <= r * LANES < high
                ],
                1,
            )
            for h in range(2):
                mine = (lane[:LANES] < HEAD_DIM) == (h == 0)
                q_one, dm_one = q_h[h][low:high], dm_h[h][low:high]
                s = mm(k, q_one, NT) + cover
                a = jnp.exp(s - lse_h[h][:, low:high])
                da = mm(v, dm_one, NT)
                ds = (a * (da - delta_h[h][:, low:high])).astype(BF)
                dv += mm(a.astype(BF), dm_one)
                dk += mm(ds, q_one)
                dq += mm(ds, jnp.where(mine, k, 0).astype(BF), TN)
            dqkv[here, pl.ds(at_k, LANES)] = dk.astype(BF)
            dqkv[here, pl.ds(at_v, LANES)] = dv.astype(BF)
            dq_sum[low:high, :] += dq
        dqkv[:, pl.ds(at_q, LANES)] = (dq_sum[...] * HEAD_DIM ** (-0.5)).astype(BF)
        return carry

    lax.fori_loop(0, width // LANES, pair, 0)
    for copy in copies:
        copy.wait()
    sum_rows = [
        mm(jnp.ones((8, length), BF), dqkv[:, part * width : (part + 1) * width])[:1, :] for part in (0, 2)
    ]
    if not grads:
        sums[...] = jnp.concatenate([*sum_rows, jnp.zeros((6, width), F32)], 0)
    out = mm(dqkv[...], wt[...]) + dr1[...]
    if fix:
        n = dr1_fix.shape[0]
        out = jnp.concatenate([out[:n] + dr1_fix[...], out[n:]], 0)
    first[...] = out[: first.shape[0]]
    if clear_first:
        out = jnp.where(lax.broadcasted_iota(jnp.int32, out.shape, 0) == 0, 0.0, out)
    dx[...] = out
    if not grads:
        return
    n_qkv, n_out = 3 * width // (PARTS * depth), width // (PARTS * depth)
    for part in range(3):
        rows = slice(part * width, (part + 1) * width)
        all_qkv[rows, :] = mm(dqkv[:, rows], x[...], TN)
    if fix:
        n = do_fix.shape[0]
        do[:n, :] = do[:n, :] + do_fix[...]
    all_out[...] = mm(do[...], mix[...], TN)
    small = jnp.concatenate([*sum_rows, jnp.zeros((6, width), F32)], 0) + sum(s[...] for s in smalls)
    up = sum(u[...] for u in ups)
    up = jnp.concatenate([up, jnp.zeros((PARTS, width - up.shape[1]), F32)], 1)
    for part in range(PARTS):
        lines[part] = up[part : part + 1]
    line = lax.broadcasted_iota(jnp.int32, (SMALL_ROWS - 8, width), 0) == 0
    for part in range(PARTS):
        place = far_place(at, part)
        for i in range(depth):
            device = i * PARTS + place
            tail = [small, jnp.where(line, lines[lax.div(device, depth) if natural else part], 0.0)]
            slab = jnp.concatenate(
                [
                    all_qkv[pl.ds(pl.multiple_of(device * n_qkv, 8), n_qkv), :],
                    all_out[pl.ds(pl.multiple_of(device * n_out, 8), n_out), :],
                    *tail,
                ],
                0,
            ).astype(BF)
            (sent if part > 3 else kept)[part % 4, i] = slab


def attention_backward(qkv, mix, lse_rows, marks, dmix, fix, far, clear_first, depth=0, at=None, smalls=(), ups=(), natural=False, wait=()):
    length, width = mix.shape
    tail = [shape(length, width, F32), shape(16, width, F32)]
    scratch = [
        pltpu.VMEM((length // LANES, 3 * LANES, LANES), F32),
        pltpu.VMEM((length, LANES), F32),
    ]
    args = [qkv, mix, lse_rows, marks[0], marks[1], dmix, *fix, *smalls, *ups]
    if depth:
        rows = 4 * width // (PARTS * depth) + SMALL_ROWS
        shapes = tail + [jax.ShapeDtypeStruct((4, depth, rows, width), BF)] * 2
        scratch += [
            pltpu.VMEM((length, 3 * width), BF), pltpu.VMEM((3 * width, width), F32), pltpu.VMEM((width, width), F32),
            pltpu.VMEM((PARTS, 1, width), F32),
        ]
        args = [at, *args]
    else:
        shapes = [shape(length, 3 * width), shape(8, width, F32)] + tail
    scratch += [pltpu.VMEM(a.shape, a.dtype) for a in far] + [pltpu.SemaphoreType.DMA((len(far),))]
    return call(
        functools.partial(attention_backward_kernel, bool(fix), clear_first, depth, natural, len(smalls)),
        shapes, scratch, 22, *args, far=far, wait=wait,
    )


def norm(values):
    centred = values - jnp.mean(values, -1, keepdims=True)
    inverse = lax.rsqrt(jnp.mean(centred * centred, -1, keepdims=True) + EPSILON)
    return centred * inverse, inverse


def norm_back(upstream, scaled, inverse, gain):
    through = upstream * gain
    return inverse * (
        through
        - jnp.mean(through, -1, keepdims=True)
        - scaled * jnp.mean(through * scaled, -1, keepdims=True)
    )


def normal_terms(u):
    size = jnp.abs(u) * (1.0 / math.sqrt(2.0))
    bell = jnp.exp(-(size * size))
    s = 1.0 / (1.0 + 0.3275911 * size)
    tail = s * (0.5 * 0.254829592 + s * (0.5 * -0.284496736 + s * (0.5 * 1.421413741 + s * (0.5 * -1.453152027 + s * (0.5 * 1.061405429)))))
    tail = tail * bell
    return jnp.where(u > 0, 1.0 - tail, tail), bell * (1.0 / math.sqrt(2.0 * math.pi))


def feed_kernel(mode, pieces_at, skip_rows, clear_first, depth, *refs):
    refs = list(refs)
    take = lambda n: [refs.pop(0) for _ in range(n)]
    (at,) = take(1) if depth else (None,)
    x, mix, w_out, vectors, up_bias = take(5)
    backward = mode != "forward"
    (cot,) = take(1) if backward else (None,)
    pieces = take(len(pieces_at))
    (y,) = take(1)
    if backward:
        do_out, dr1_out, dm_out, small, up_small = take(5)
        if mode == "rows":
            n1_s, g_s, du_s, df_s = take(4)
        elif mode == "order":
            (whole,) = take(1)
        else:
            sent, kept = take(2)
    slabs, sems, z1_s, q1_s = take(4)
    if backward:
        (slope,) = take(1)
        if mode != "rows":
            n1_s, g_s, du_s, df_s, stage, out_sems = take(6)
        small[...] = jnp.zeros_like(small)
        up_small[...] = jnp.zeros_like(up_small)
    else:
        (n1_s,) = take(1)
    count, width = y.shape
    half = slabs.shape[1] // 2
    each = slabs.shape[0] // PARTS
    copies = []
    for i, (piece, begin) in enumerate(zip(pieces, pieces_at)):
        copies.append(
            pltpu.make_async_copy(
                piece.at[:, pl.ds(skip_rows, 2 * half), :], slabs.at[pl.ds(begin, piece.shape[0])], sems.at[i]
            )
        )
        copies[-1].start()

    def weights(part, lower):
        top = half if lower else 0
        return slabs[part * each : (part + 1) * each, top : top + half, :].reshape(each * half, width)

    b_out, b_down, shift_one, shift_two, gain_one, gain_two = (vectors[i : i + 1, :] for i in range(2, 8))
    r1 = x[:count, :].astype(F32) + mm(mix[:count, :], w_out[...], NT) + b_out
    z1, q1 = norm(r1)
    z1_s[...] = z1
    q1_s[...] = q1
    n1_s[...] = (z1 * gain_one + shift_one).astype(BF)
    for copy in copies:
        copy.wait()
    tile = min(256, count)

    def rows_step(i, carry):
        here = pl.ds(pl.multiple_of(i * tile, tile), tile)
        n1 = n1_s[here, :]
        acc = n1.astype(F32) + b_down
        for part in range(PARTS):
            u = mm(n1, weights(part, False), NT) + up_bias[part : part + 1, :]
            size = u.shape[1]
            cols = slice(part * size, (part + 1) * size)
            big, bell = normal_terms(u)
            g = (u * big).astype(BF)
            if backward:
                g_s[here, cols] = g
                slope[:, cols] = big + u * bell
            acc += mm(g, weights(part, True))
        z2, q2 = norm(acc)
        y[here, :] = (z2 * gain_two + shift_two).astype(BF)
        if backward:
            e = cot[here, :].astype(F32)
            if clear_first:
                e = jnp.where(lax.broadcasted_iota(jnp.int32, e.shape, 0) + i * tile == 0, 0.0, e)
            small[5:6, :] += jnp.sum(e, 0, keepdims=True)
            small[7:8, :] += jnp.sum(e * z2, 0, keepdims=True)
            dr2 = norm_back(e, z2, q2, gain_two)
            df = dr2.astype(BF)
            df_s[here, :] = df
            small[3:4, :] += jnp.sum(df.astype(F32), 0, keepdims=True)
            dn1 = dr2
            for part in range(PARTS):
                da = mm(df, weights(part, True), NT)
                size = da.shape[1]
                cols = slice(part * size, (part + 1) * size)
                du = (da * slope[:, cols]).astype(BF)
                du_s[here, cols] = du
                up_small[part : part + 1, :] += jnp.sum(du.astype(F32), 0, keepdims=True)
                dn1 += mm(du, weights(part, False))
            z1 = z1_s[here, :]
            small[4:5, :] += jnp.sum(dn1, 0, keepdims=True)
            small[6:7, :] += jnp.sum(dn1 * z1, 0, keepdims=True)
            dr1 = norm_back(dn1, z1, q1_s[here, :], gain_one)
            do = dr1.astype(BF)
            small[2:3, :] += jnp.sum(do.astype(F32), 0, keepdims=True)
            dm_out[here, :] = mm(do, w_out[...]).astype(BF)
            do_out[here, :] = do
            dr1_out[here, :] = dr1
        return carry

    lax.fori_loop(0, count // tile, rows_step, 0)
    if mode not in ("order", "spread"):
        return
    for part in range(PARTS):
        slot = part % 2
        if part > 1:
            for i in range(depth):
                pltpu.make_async_copy(stage.at[slot, i], stage.at[slot, i], out_sems.at[slot, i]).wait()
        size = g_s.shape[1] // PARTS
        cols = slice(part * size, (part + 1) * size)
        for lower, (left, right) in enumerate(((du_s, n1_s), (g_s, df_s))):
            full = mm(left[:, cols], right[...], TN).astype(BF).reshape(depth, half, width)
            stage[slot, :, lower * half : (lower + 1) * half, :] = full
        for i in range(depth):
            src, sem = stage.at[slot, i], out_sems.at[slot, i]
            if mode == "order":
                pltpu.make_async_copy(src, whole.at[i * PARTS + far_place(at, part)], sem).start()
            else:
                device = part * depth + i
                z, y_bit, x_bit, core_bit = device // PARTS, device // 4 % 2, device // 2 % 2, device % 2
                code = (at[0] ^ y_bit) + 2 * (at[1] ^ x_bit)

                @pl.when(at[2] == core_bit)
                def _():
                    pltpu.make_async_copy(src, kept.at[code, z], sem).start()

                @pl.when(at[2] != core_bit)
                def _():
                    pltpu.make_async_copy(src, sent.at[code, z], sem).start()

    for slot in range(2):
        for i in range(depth):
            pltpu.make_async_copy(stage.at[slot, i], stage.at[slot, i], out_sems.at[slot, i]).wait()


def feed(mode, x, mix, w_out, vectors, up_bias, pieces, pieces_at, cot=None, count=None, clear_first=False, skip_rows=0, depth=0, at=None, wait=()):
    width = x.shape[1]
    count = count or x.shape[0]
    hidden = PARTS * up_bias.shape[1]
    wide, high = shape(count, width), shape(count, hidden)
    rows = pieces[0].shape[1] - skip_rows
    tile = min(256, count)
    shapes = [wide]
    scratch = [
        pltpu.VMEM((2 * hidden // rows, rows, width), BF), pltpu.SemaphoreType.DMA((len(pieces),)),
        pltpu.VMEM((count, width), F32), pltpu.VMEM((count, 1), F32),
    ]
    args = [x, mix, w_out, vectors, up_bias]
    far_outs = 0
    kept = [wide, high, high, wide]
    in_vmem = [pltpu.VMEM(k.shape, BF) for k in kept]
    if mode == "forward":
        scratch.append(in_vmem[0])
    else:
        args.append(cot)
        shapes += [wide, shape(count, width, F32), wide, shape(8, width, F32), shape(*up_bias.shape, F32)]
        scratch.append(pltpu.VMEM((tile, hidden), F32))
        if mode == "rows":
            shapes += kept
        else:
            scratch += in_vmem + [pltpu.VMEM((2, depth, rows, width), BF), pltpu.SemaphoreType.DMA((2, depth))]
            out = lambda *lead: jax.ShapeDtypeStruct((*lead, rows, width), BF)
            outs = [out(PARTS * depth)] if mode == "order" else [out(4, depth), out(4, depth)]
            shapes += outs
            far_outs = len(outs)
            args = [at, *args]
    return call(
        functools.partial(feed_kernel, mode, pieces_at, skip_rows, clear_first, depth),
        shapes, scratch, 40 if count > 16 else 12, *args, far=pieces, far_outs=far_outs, wait=wait,
    )


def feed_grads_kernel(first, layout, halves, received, *refs):
    refs = list(refs)
    n1, df, g, du = (refs[i * halves : (i + 1) * halves] for i in range(4))
    refs = refs[4 * halves :]
    got = [refs.pop(0) for _ in range(received)]
    stacked = layout is None
    for index in range(refs[0].shape[0] if stacked else len(layout)):
        part = first + index
        outs = [refs[0].at[index]] if stacked else [refs.pop(0) for _ in range(layout[index])]
        size = g[0].shape[1] // PARTS
        cols = slice(part * size, (part + 1) * size)
        for lower, (left, right) in enumerate(((du, n1), (g, df))):
            full = sum(mm(a[:, cols], b[...], TN) for a, b in zip(left, right))
            at = 0
            for out in outs:
                slabs, half = out.shape[0], out.shape[1] // 2
                rows = slice(lower * half, (lower + 1) * half)
                value = full[at * half : (at + slabs) * half].reshape(slabs, half, out.shape[2])
                if received:
                    value += got[0][index, at : at + slabs, rows, :].astype(F32)
                out[:, rows, :] = value.astype(BF)
                at += slabs


def feed_grads(first, shapes, layout, n1, df, g, du, *received):
    width = n1[0].shape[1]
    outs = [jax.ShapeDtypeStruct((*lead, width), BF) for lead in shapes]
    return call(
        functools.partial(feed_grads_kernel, first, layout, len(n1), len(received)),
        outs, [], 8, *n1, *df, *g, *du, *received,
    )


def add_parts_kernel(kept, received, here, by_y, by_x, both_a, both_b):
    half = both_a.shape[0]
    for part, out in enumerate((here, by_y, by_x)):
        out[...] = kept[part] + received[part]
    both_a[...] = kept[3, :half] + received[3, :half]
    both_b[...] = kept[3, half:] + received[3, half:]


def add_parts(kept, received, wait=()):
    depth, rows, width = kept.shape[1:]
    out = lambda n: jax.ShapeDtypeStruct((n, rows, width), BF)
    shapes = [out(depth), out(depth), out(depth), out(depth // 2), out(depth // 2)]
    return call(add_parts_kernel, shapes, [], 4, kept, received, wait=wait)


def join_kernel(one, one_y, one_x, two, two_y, two_x, out):
    rows = one.shape[1]
    out[:, :rows, :] = one[...] + one_y[...] + one_x[...]
    out[:, rows:, :] = two[...] + two_y[...] + two_x[...]


def join(one, two, wait=()):
    depth, rows, width = one[0].shape
    return call(join_kernel, [jax.ShapeDtypeStruct((depth, 2 * rows, width), BF)], [], 3, *one, *two, wait=wait)[0]


def after(values, *before):
    return lax.optimization_barrier((values, before))[0]


def swap(array, axis):
    return lax.ppermute(array, axis, [(0, 1), (1, 0)])


def swaps(arrays, axis):
    return [swap(a, axis) for a in arrays]


def marks_of(lengths, segments):
    length = segments.shape[1]
    place = lax.broadcasted_iota(jnp.int32, (1, length), 1)
    keys = jnp.where(place < lengths[:, None], segments, -1)
    return segments, keys.reshape(length, 1)


class Near:
    axes = ("z", "y", "x", "core")

    def __init__(self, shards):
        self.shards = shards
        self.depth = lax.axis_size("z")
        y, x, core = (lax.axis_index(name) for name in self.axes[1:])
        self.at = jnp.stack([y, x, core])
        self.z = lax.axis_index("z")
        self.device = self.z * PARTS + y * 4 + x * 2 + core
        w_qkv, w_out, w_up = shards[:3]
        self.n_qkv, self.n_out, self.n_up = w_qkv.shape[2], w_out.shape[2], w_up.shape[2]
        half = self.depth // 2
        own = [(0, 0), (1, 0), (2, 0), (3, 0), (3, half)]
        self.slabs = own + [(part + 4, first) for part, first in own]

    def slab_pair(self, index):
        w_qkv, w_out, w_up, w_down, biases, gains, up_bias = (s[index] for s in self.shards)
        width = w_qkv.shape[0]
        natural = lax.dynamic_update_slice(
            jnp.zeros((8, width), BF), jnp.concatenate([biases, gains], 0), (0, self.device * self.n_out)
        )
        line = lax.dynamic_update_slice(jnp.zeros((8, width), BF), up_bias[None], (0, self.z * self.n_up))
        attention = jnp.concatenate([w_qkv.T, w_out.T, natural, line], 0)
        return attention, jnp.concatenate([w_up.T, w_down], 0)

    def along_z(self, slab):
        return lax.all_gather(slab, "z", axis=0, tiled=False)

    def near(self, here):
        return [here, swap(here, "y"), swap(here, "x")]

    def diagonal(self, near):
        half = self.depth // 2
        return [swap(near[1][:half], "x"), swap(near[2][half:], "y")]

    def attend(self, x, marks, pieces):
        slabs = self.slabs if len(pieces) > 1 else []
        out = attention_forward(x, marks, pieces, self.at, slabs, self.depth, self.n_up)
        return dict(zip(("x", "qkv", "mix", "lse", "wt", "wt_out", "small", "up_bias"), [x, *out]))

    def feed(self, mode, kept, pieces, cot, count=None, clear_first=False, wait=()):
        if len(pieces) > 1:
            pieces_at = [part * self.depth + first for part, first in self.slabs]
        else:
            pieces_at = [0]
        grads = mode != "rows"
        out = feed(
            mode, kept["x"], kept["mix"], kept["wt_out"], kept["small"], kept["up_bias"], pieces, pieces_at,
            cot, count, clear_first, pieces[0].shape[1] - 2 * self.n_up,
            self.depth if grads else 0, self.at if grads else None, wait,
        )
        last = {"rows": ("n1", "g", "du", "df"), "order": ("all",), "spread": ("sent", "kept")}[mode]
        return dict(zip(("y", "do", "dr1", "dm", "small", "up") + last, out))

    def reduce_diagonal(self, both):
        return [swap(both[0], "x"), swap(both[1], "y")]

    def add_diagonal(self, by_y, by_x, got):
        half = self.depth // 2
        return [by_y.at[:half].add(got[0]), by_x.at[half:].add(got[1])]

    def reduce_near(self, added):
        return [swap(added[0], "y"), swap(added[1], "x")]

    def reduce_z(self, here, got):
        return lax.psum_scatter(here + got[0] + got[1], "z", scatter_dimension=0, tiled=False)

    def attend_back(self, kept, marks, back, fix, clear_first, natural, wait=()):
        smalls, ups = [f["small"] for f in [back, *fix]], [f["up"] for f in [back, *fix]]
        return attention_backward(
            kept["qkv"], kept["mix"], kept["lse"], marks, back["dm"], [f[n] for f in fix for n in ("dm", "dr1", "do")],
            [kept["wt"], back["dr1"], kept["x"], back["do"]], clear_first, self.depth, self.at, smalls, ups, natural, wait,
        )

    def attention_outs(self, total, natural):
        total = total.astype(F32)
        n_qkv, n_out, n_up = self.n_qkv, self.n_out, self.n_up
        small = total[n_qkv + n_out :]
        own = lax.dynamic_slice(small, (0, self.device * n_out), (8, n_out))
        up = lax.dynamic_slice(small, (8, (self.device % self.depth if natural else self.z) * n_up), (1, n_up))[0]
        return total[:n_qkv].T, total[n_qkv : n_qkv + n_out].T, own[:6], own[6:], up

    def first_row_terms(self, fix):
        width = fix["n1"].shape[1]
        rows = jnp.stack([fix["n1"][0], fix["df"][0]]).reshape(1, 2 * width)
        table = jnp.stack([fix["du"][0].reshape(PARTS, self.depth, self.n_up), fix["g"][0].reshape(PARTS, self.depth, self.n_up)], 2)
        table = table.reshape(1, PARTS, -1)
        for axis in ("core", "x", "y"):
            n, far = table.shape[0], table.shape[1] // 2
            flat = jnp.concatenate([rows, table[:, far:].reshape(n, -1)], 1)
            got = swap(flat, axis)
            rows = jnp.concatenate([rows, got[:, : 2 * width]], 0)
            table = jnp.concatenate([table[:, :far], got[:, 2 * width :].reshape(n, far, -1)], 0)
        n = rows.shape[0]
        flat = jnp.concatenate([rows, table.reshape(n, -1)], 1)
        step = 1
        while step < self.depth:
            pairs = [(i, i ^ step) for i in range(self.depth)]
            flat = jnp.concatenate([flat, lax.ppermute(flat, "z", pairs)], 0)
            step *= 2
        own = flat[:, 2 * width :].reshape(flat.shape[0], self.depth, 2, self.n_up)
        own = lax.dynamic_index_in_dim(own, self.z, 1, keepdims=False)
        up = mm(own[:, 0], flat[:, :width], TN)
        down = mm(own[:, 1], flat[:, width : 2 * width], TN)
        return up, down


def near_body(tokens, skip_tokens, cot_first, cot_second, *rest):
    *shards, lengths, segments = rest
    link = Near(shards)
    marks = marks_of(lengths, segments)
    length = segments.shape[1]
    is_first = lax.broadcasted_iota(jnp.int32, (length, 1), 0) == 0

    slab_a1, slab_m1 = link.slab_pair(0)
    a1 = link.along_z(slab_a1)
    m1 = link.along_z(slab_m1)
    b2 = [lax.all_gather(after(jnp.concatenate(link.slab_pair(1), 0), a1), link.axes, axis=0, tiled=False)]
    a1 = link.near(a1)
    a1 += link.diagonal(a1)
    m1 = link.near(after(m1, a1[:3]))
    a1 += swaps(a1, "core")
    one = link.attend(*after((tokens, marks, a1), m1[0]))
    m1 = after(m1, one["mix"])
    m1 += link.diagonal(m1)
    m1 += swaps(m1, "core")
    back_one = link.feed("order", one, m1, cot_first, None, True)
    sum_m1 = lax.psum_scatter(back_one["all"], link.axes, scatter_dimension=0, tiled=False)
    out_first = back_one["y"]
    second_in = jnp.where(is_first, out_first, skip_tokens)
    two = link.attend(second_in, marks, b2)
    back_two = link.feed("spread", two, b2, cot_second)
    received_m2 = swap(back_two["sent"], "core")
    grad_skip, first2, sent_a2, kept_a2 = link.attend_back(two, marks, back_two, [], True, True)
    kept_m2, received_m2, sent_a2, kept_a2 = after((back_two["kept"], received_m2, sent_a2, kept_a2), first2)
    received_a2 = swap(sent_a2, "core")
    kept_m2 = add_parts(kept_m2, received_m2)
    got_m2 = link.reduce_diagonal(kept_m2[3:])
    kept_a2 = add_parts(kept_a2, received_a2)
    got_a2 = link.reduce_diagonal(kept_a2[3:])
    upstream = jnp.where(is_first[:16], cot_first[:16].astype(F32) + first2, 0.0)
    fix = link.feed("rows", one, m1, after(upstream, kept_m2, kept_a2), 16)
    kept_m2, got_m2, kept_a2, got_a2 = after((kept_m2, got_m2, kept_a2, got_a2), fix["y"])
    added_m2 = link.add_diagonal(*kept_m2[1:3], got_m2)
    got_m2 = link.reduce_near(added_m2)
    grad_tokens, _, sent_a1, kept_a1 = link.attend_back(
        one, marks, *after((back_one, [fix]), added_m2), False, False
    )
    kept_m2, got_m2, kept_a2, got_a2, sent_a1, sum_m1 = after(
        (kept_m2, got_m2, kept_a2, got_a2, sent_a1, sum_m1), kept_a1
    )
    received_a1 = swap(sent_a1, "core")
    sum_m2 = link.reduce_z(kept_m2[0], got_m2)
    got_a2 = link.reduce_near(link.add_diagonal(*kept_a2[1:3], got_a2))
    kept_a1 = add_parts(kept_a1, received_a1)
    got_a1 = link.reduce_diagonal(kept_a1[3:])
    got_a1 = link.reduce_near(link.add_diagonal(*kept_a1[1:3], got_a1))
    fix = after(fix, kept_a1)
    both = join([kept_a1[0], *got_a1], [kept_a2[0], *got_a2], [sum_m2])
    both = lax.psum_scatter(both, "z", scatter_dimension=0, tiled=False)
    sum_a1, sum_a2 = both[: both.shape[0] // 2], both[both.shape[0] // 2 :]

    n_up = link.n_up
    up_fix, down_fix = link.first_row_terms(fix)
    sum_m1, sum_m2 = sum_m1.astype(F32), sum_m2.astype(F32)
    outs = [link.attention_outs(sum_a1, False), link.attention_outs(sum_a2, True)]
    pair = lambda i: jnp.stack([outs[0][i], outs[1][i]])
    return (
        out_first, back_two["y"], grad_tokens, grad_skip,
        pair(0), pair(1),
        jnp.stack([(sum_m1[:n_up] + up_fix).T, sum_m2[:n_up].T]),
        jnp.stack([sum_m1[n_up:] + down_fix, sum_m2[n_up:]]),
        pair(2), pair(3), pair(4),
    )


def far_body(tokens, skip_tokens, cot_first, cot_second, *rest):
    *shards, lengths, segments = rest
    axes = ("wide", "narrow")
    devices = lax.axis_size("wide") * lax.axis_size("narrow")
    marks = marks_of(lengths, segments)
    length, width = tokens.shape
    is_first = lax.broadcasted_iota(jnp.int32, (length, 1), 0) == 0
    gather = lambda a: lax.all_gather(a, axes, axis=0, tiled=True)
    scatter = lambda a: lax.psum_scatter(a, axes, scatter_dimension=0, tiled=True)

    def fetch(index):
        w_qkv, w_out, w_up, w_down, biases, gains, up_bias = (s[index] for s in shards)
        small = gather(jnp.concatenate([biases, gains], 0).T).T.astype(F32)
        up, down = (gather(w).reshape(PARTS, -1, width) for w in (w_up.T, w_down))
        both = jnp.concatenate([up, down], 1)
        return (
            gather(w_qkv.T), gather(w_out.T), small, gather(up_bias).astype(F32).reshape(PARTS, -1),
            [both],
        )

    def forward(x, weights):
        wt, wt_out, small, up_bias, pieces = weights
        qkv, mix, lse = attention_forward(x, marks, (wt, small))
        return (qkv, mix, lse), feed("forward", x, mix, wt_out, small, up_bias, pieces, [0])[0]

    def backward(x, weights, kept, cot, clear_first):
        wt, wt_out, small, up_bias, pieces = weights
        qkv, mix, lse = kept
        y, do, dr1, dm, sums, up_sums, n1, g, du, df = feed("rows", x, mix, wt_out, small, up_bias, pieces, [0], cot)
        dqkv, more, dx, first = attention_backward(qkv, mix, lse, marks, dm, [], [wt, dr1], clear_first)
        rows = 2 * up_bias.shape[1]
        lists = [[n1], [df], [g], [du]]
        parts = jnp.concatenate([feed_grads(i, [(4, 1, rows)], None, *lists)[0][:, 0] for i in (0, 4)], 0)
        up, down = (p.reshape(-1, width) for p in (parts[:, : rows // 2], parts[:, rows // 2 :]))
        sums = scatter((sums + more).T).T
        grads = (
            scatter(mm(dqkv, x, TN).astype(BF)).astype(F32).T,
            scatter(mm(do, mix, TN).astype(BF)).astype(F32).T,
            scatter(up).astype(F32).T,
            scatter(down).astype(F32),
            sums[:6], sums[6:], scatter(up_sums.reshape(-1)),
        )
        return y, dx, first, grads

    one, two = fetch(0), fetch(1)
    kept_one, out_first = forward(tokens, one)
    second_in = jnp.where(is_first, out_first, skip_tokens)
    kept_two, _ = forward(second_in, two)
    out_second, grad_skip, first, grads_two = backward(second_in, two, kept_two, cot_second, True)
    first = jnp.concatenate([first, jnp.zeros((length - first.shape[0], width), F32)], 0)
    upstream = cot_first.astype(F32) + jnp.where(is_first, first, 0.0)
    _, grad_tokens, _, grads_one = backward(tokens, one, kept_one, upstream, False)
    return (out_first, out_second, grad_tokens, grad_skip, *(jnp.stack(p) for p in zip(grads_one, grads_two)))


def solution(mesh):
    wide, narrow = mesh.shape["wide"], mesh.shape["narrow"]
    if narrow == 4 and wide % 4 == 0:
        mesh = Mesh(mesh.devices.reshape(wide // 2, 2, 2, 2), Near.axes)
        body, every = near_body, Near.axes
    else:
        body, every = far_body, ("wide", "narrow")
    rows, last, middle = P(every, None), P(None, None, every), P(None, every, None)
    return jax.shard_map(
        body,
        mesh=mesh,
        in_specs=(
            rows, rows, rows, rows, last, last, last, middle, last, last, P(None, every), P(every), rows,
        ),
        out_specs=(rows, rows, rows, rows, last, last, last, middle, last, last, P(None, every)),
        check_vma=False,
    )
```

```python
import functools
import math

import jax
import jax.numpy as jnp
from jax import lax
from jax.experimental import pallas as pl
from jax.experimental.pallas import tpu as pltpu
from jax.sharding import Mesh, PartitionSpec as P

HEADS = 12
HEAD_DIM = 64
EPSILON = 1e-12
MASKED = -1e30
BF = jnp.bfloat16
F32 = jnp.float32
NT = (((1,), (1,)), ((), ()))
TN = (((0,), (0,)), ((), ()))
NN = (((1,), (0,)), ((), ()))
PARTS = 8
LANES = 128
SMALL_ROWS = 16
VMEM = pl.BlockSpec(memory_space=pltpu.VMEM)
SMEM = pl.BlockSpec(memory_space=pltpu.SMEM)


def mm(a, b, dims=NN):
    return lax.dot_general(a, b, dims, preferred_element_type=F32)


def shape(rows, cols, dtype=BF):
    return jax.ShapeDtypeStruct((rows, cols), dtype)


def call(kernel, out_shapes, scratch, work, *args, far=(), far_outs=0, wait=()):
    before, ahead = len(args) + len(far), len(wait)
    inner = kernel
    kernel = lambda *refs: inner(*refs[:before], *refs[before + ahead :])
    return list(pl.pallas_call(
        kernel,
        out_shape=out_shapes,
        in_specs=[SMEM if a.ndim == 1 else VMEM for a in args] + [pl.BlockSpec(memory_space=pl.ANY)] * (len(far) + ahead),
        out_specs=[VMEM] * (len(out_shapes) - far_outs) + [pl.BlockSpec(memory_space=pl.ANY)] * far_outs,
        scratch_shapes=scratch,
        compiler_params=pltpu.CompilerParams(vmem_limit_bytes=VMEM_BYTES),
        cost_estimate=pl.CostEstimate(flops=int(work * 1.15e9), bytes_accessed=0, transcendentals=0),
    )(*args, *far, *wait))


VMEM_BYTES = 56 * 1024 * 1024


def windows(length):
    tiles = length // LANES
    return [
        (t, max(0, t - 1) * LANES, min(tiles, t + 2) * LANES) for t in range(tiles)
    ]


def far_place(at, part):
    return (at[0] ^ (part % 2)) * 4 + (at[1] ^ (part // 2 % 2)) * 2 + (at[2] ^ (part // 4))


def assemble(slabs, depth, at, pieces, wt, wt_out, small, up_bias, all_qkv, all_out, landing, sems):
    width = wt.shape[1]
    n_qkv, n_out = 3 * width // (PARTS * depth), width // (PARTS * depth)
    rest = n_qkv + n_out
    rows = landing.shape[1]
    copies, done = [], 0
    for i, piece in enumerate(pieces):
        n = piece.shape[0]
        copies.append(pltpu.make_async_copy(piece.at[:, pl.ds(0, rows), :], landing.at[pl.ds(done, n)], sems.at[i]))
        copies[-1].start()
        done += n
    small[...] = jnp.zeros_like(small)
    up_bias[...] = jnp.zeros_like(up_bias)
    done = 0
    for index, (piece, copy) in enumerate(zip(pieces, copies)):
        copy.wait()
        for i in range(piece.shape[0]):
            if slabs:
                part, first = slabs[index]
                device = (first + i) * PARTS + far_place(at, part)
            else:
                part, device = i // depth, i
            slab = landing[done].astype(F32)
            done += 1
            all_qkv[pl.ds(pl.multiple_of(device * n_qkv, 8), n_qkv), :] = slab[:n_qkv]
            all_out[pl.ds(pl.multiple_of(device * n_out, 8), n_out), :] = slab[n_qkv:rest]
            small[...] += slab[rest : rest + 8]
            line = slab[rest + 8 : rest + 9]
            if not slabs:
                shift = (i % depth - i // PARTS) * (up_bias.shape[1] // depth)
                line = pltpu.roll(line, shift % width, 1)
            up_bias[part : part + 1, :] += line[:, : up_bias.shape[1]]
    wt[...] = all_qkv[...].astype(BF)
    wt_out[...] = all_out[...].astype(BF)


def attention_forward_kernel(slabs, depth, x, seg_row, key_col, *refs):
    refs = list(refs)
    length, width = x.shape
    if slabs is None:
        wt, small, qkv, mix, lse_rows, mask = refs
    else:
        count = len(slabs) or 1
        at, pieces, refs = refs[0], refs[1 : 1 + count], refs[1 + count :]
        qkv, mix, lse_rows, wt, wt_out, small, up_bias, mask, all_qkv, all_out, landing, sems = refs
        assemble(slabs, depth, at, pieces, wt, wt_out, small, up_bias, all_qkv, all_out, landing, sems)
    for part in range(3):
        cols = slice(part * width, (part + 1) * width)
        out = mm(x[...], wt[cols, :], NT)
        if part != 1:
            out += small[part // 2 : part // 2 + 1, :]
        qkv[:, cols] = out.astype(BF)
    for t, low, high in windows(length):
        keys = lax.broadcasted_iota(jnp.int32, (high - low, LANES), 0) + low
        rows = lax.broadcasted_iota(jnp.int32, (high - low, LANES), 1) + t * LANES
        same = key_col[low:high, :] == seg_row[:, t * LANES : (t + 1) * LANES]
        mask[t, : high - low, :] = jnp.where(same | (rows == keys), 0.0, MASKED)

    def pair(p, carry):
        at_q = pl.multiple_of(p * LANES, LANES)
        at_k = pl.multiple_of(at_q + width, LANES)
        at_v = pl.multiple_of(at_q + 2 * width, LANES)
        lane = lax.broadcasted_iota(jnp.int32, (LANES, LANES), 1)
        for t, low, high in windows(length):
            here = slice(t * LANES, (t + 1) * LANES)
            q = qkv[here, pl.ds(at_q, LANES)] * HEAD_DIM ** (-0.5)
            k = qkv[low:high, pl.ds(at_k, LANES)]
            v = qkv[low:high, pl.ds(at_v, LANES)]
            outs = []
            for h in range(2):
                mine = (lane < HEAD_DIM) == (h == 0)
                s = mm(k, jnp.where(mine, q, 0).astype(BF), NT) + mask[t, : high - low, :]
                top = jnp.max(s, 0, keepdims=True)
                e = jnp.exp(s - top)
                total = jnp.sum(e, 0, keepdims=True)
                outs.append(mm((e * (1.0 / total)).astype(BF), v, TN))
                lse_rows[2 * p + h, :, here] = top + jnp.log(total)
            mix[here, pl.ds(at_q, LANES)] = jnp.where(lane < HEAD_DIM, outs[0], outs[1]).astype(BF)
        return carry

    lax.fori_loop(0, width // LANES, pair, 0)


def attention_forward(x, marks, weights, at=None, slabs=None, depth=0, rows_up=0):
    length, width = x.shape
    shapes = [shape(length, 3 * width), shape(length, width), jax.ShapeDtypeStruct((HEADS, 1, length), F32)]
    scratch = [pltpu.VMEM((length // LANES, 3 * LANES, LANES), F32)]
    args, far = list(weights), []
    if slabs is not None:
        args, far = [at], args
        shapes += [
            shape(3 * width, width), shape(width, width), shape(8, width, F32), shape(PARTS, depth * rows_up, F32),
        ]
        rows = 4 * width // (PARTS * depth) + SMALL_ROWS
        scratch += [
            pltpu.VMEM((3 * width, width), F32), pltpu.VMEM((width, width), F32),
            pltpu.VMEM((PARTS * depth, rows, width), BF), pltpu.SemaphoreType.DMA((len(far),)),
        ]
    return call(
        functools.partial(attention_forward_kernel, slabs, depth),
        shapes, scratch, 15, x, marks[0], marks[1], *args, far=far,
    )


def attention_backward_kernel(fix, clear_first, depth, natural, n_small, *refs):
    refs = list(refs)
    take = lambda n: [refs.pop(0) for _ in range(n)]
    grads = depth > 0
    (at,) = take(1) if grads else (None,)
    qkv, mix, lse_rows, seg_row, key_col, dmix = take(6)
    dmix_fix, dr1_fix = take(2) if fix else (None, None)
    (do_fix,) = take(1) if fix and grads else (None,)
    smalls, ups = take(n_small), take(n_small)
    far = take(4 if grads else 2)
    if grads:
        dx, first, sent, kept, mask, dq_sum, dqkv, all_qkv, all_out, lines, *near, sems = refs
        wt, dr1, x, do = near
    else:
        dqkv, sums, dx, first, mask, dq_sum, *near, sems = refs
        wt, dr1 = near
    copies = [pltpu.make_async_copy(a, b, sems.at[i]) for i, (a, b) in enumerate(zip(far, near))]
    for copy in copies:
        copy.start()
    length, width = mix.shape
    for t, low, high in windows(length):
        keys = lax.broadcasted_iota(jnp.int32, (high - low, LANES), 0) + low
        rows = lax.broadcasted_iota(jnp.int32, (high - low, LANES), 1) + t * LANES
        same = key_col[low:high, :] == seg_row[:, t * LANES : (t + 1) * LANES]
        mask[t, : high - low, :] = jnp.where(same | (rows == keys), 0.0, MASKED)

    def pair(p, carry):
        at_q = pl.multiple_of(p * LANES, LANES)
        at_k = pl.multiple_of(at_q + width, LANES)
        at_v = pl.multiple_of(at_q + 2 * width, LANES)
        lane = lax.broadcasted_iota(jnp.int32, (length, LANES), 1)
        q = qkv[:, pl.ds(at_q, LANES)] * HEAD_DIM ** (-0.5)
        dm = dmix[:, pl.ds(at_q, LANES)]
        if fix:
            n = dmix_fix.shape[0]
            dm = jnp.concatenate([dm[:n] + dmix_fix[:, pl.ds(at_q, LANES)], dm[n:]], 0)
        product = dm.astype(F32) * mix[:, pl.ds(at_q, LANES)].astype(F32)
        ones_lane = lax.broadcasted_iota(jnp.int32, (8, LANES), 1)
        q_h, dm_h, lse_h, delta_h = [], [], [], []
        for h in range(2):
            mine = (lane < HEAD_DIM) == (h == 0)
            q_h.append(jnp.where(mine, q, 0).astype(BF))
            dm_h.append(jnp.where(mine, dm, 0).astype(BF))
            picks = jnp.where((ones_lane < HEAD_DIM) == (h == 0), 1.0, 0.0)
            delta_h.append(
                lax.dot_general(picks, product, NT, precision=lax.Precision.HIGHEST, preferred_element_type=F32)[:1, :]
            )
            lse_h.append(lse_rows[2 * p + h])
        dq_sum[...] = jnp.zeros_like(dq_sum)
        for t, low, high in windows(length):
            here = slice(t * LANES, (t + 1) * LANES)
            k = qkv[here, pl.ds(at_k, LANES)]
            v = qkv[here, pl.ds(at_v, LANES)]
            dk = jnp.zeros((LANES, LANES), F32)
            dv = jnp.zeros((LANES, LANES), F32)
            dq = jnp.zeros((high - low, LANES), F32)
            cover = jnp.concatenate(
                [
                    mask[r, t * LANES - low_r : (t + 1) * LANES - low_r, :]
                    for r, low_r, _ in windows(length)
                    if low <= r * LANES < high
                ],
                1,
            )
            for h in range(2):
                mine = (lane[:LANES] < HEAD_DIM) == (h == 0)
                q_one, dm_one = q_h[h][low:high], dm_h[h][low:high]
                s = mm(k, q_one, NT) + cover
                a = jnp.exp(s - lse_h[h][:, low:high])
                da = mm(v, dm_one, NT)
                ds = (a * (da - delta_h[h][:, low:high])).astype(BF)
                dv += mm(a.astype(BF), dm_one)
                dk += mm(ds, q_one)
                dq += mm(ds, jnp.where(mine, k, 0).astype(BF), TN)
            dqkv[here, pl.ds(at_k, LANES)] = dk.astype(BF)
            dqkv[here, pl.ds(at_v, LANES)] = dv.astype(BF)
            dq_sum[low:high, :] += dq
        dqkv[:, pl.ds(at_q, LANES)] = (dq_sum[...] * HEAD_DIM ** (-0.5)).astype(BF)
        return carry

    lax.fori_loop(0, width // LANES, pair, 0)
    for copy in copies:
        copy.wait()
    sum_rows = [
        mm(jnp.ones((8, length), BF), dqkv[:, part * width : (part + 1) * width])[:1, :] for part in (0, 2)
    ]
    if not grads:
        sums[...] = jnp.concatenate([*sum_rows, jnp.zeros((6, width), F32)], 0)
    out = mm(dqkv[...], wt[...]) + dr1[...]
    if fix:
        n = dr1_fix.shape[0]
        out = jnp.concatenate([out[:n] + dr1_fix[...], out[n:]], 0)
    first[...] = out[: first.shape[0]]
    if clear_first:
        out = jnp.where(lax.broadcasted_iota(jnp.int32, out.shape, 0) == 0, 0.0, out)
    dx[...] = out
    if not grads:
        return
    n_qkv, n_out = 3 * width // (PARTS * depth), width // (PARTS * depth)
    for part in range(3):
        rows = slice(part * width, (part + 1) * width)
        all_qkv[rows, :] = mm(dqkv[:, rows], x[...], TN)
    if fix:
        n = do_fix.shape[0]
        do[:n, :] = do[:n, :] + do_fix[...]
    all_out[...] = mm(do[...], mix[...], TN)
    small = jnp.concatenate([*sum_rows, jnp.zeros((6, width), F32)], 0) + sum(s[...] for s in smalls)
    up = sum(u[...] for u in ups)
    up = jnp.concatenate([up, jnp.zeros((PARTS, width - up.shape[1]), F32)], 1)
    for part in range(PARTS):
        lines[part] = up[part : part + 1]
    line = lax.broadcasted_iota(jnp.int32, (SMALL_ROWS - 8, width), 0) == 0
    for part in range(PARTS):
        place = far_place(at, part)
        for i in range(depth):
            device = i * PARTS + place
            tail = [small, jnp.where(line, lines[lax.div(device, depth) if natural else part], 0.0)]
            slab = jnp.concatenate(
                [
                    all_qkv[pl.ds(pl.multiple_of(device * n_qkv, 8), n_qkv), :],
                    all_out[pl.ds(pl.multiple_of(device * n_out, 8), n_out), :],
                    *tail,
                ],
                0,
            ).astype(BF)
            (sent if part > 3 else kept)[part % 4, i] = slab


def attention_backward(qkv, mix, lse_rows, marks, dmix, fix, far, clear_first, depth=0, at=None, smalls=(), ups=(), natural=False, wait=()):
    length, width = mix.shape
    tail = [shape(length, width, F32), shape(16, width, F32)]
    scratch = [
        pltpu.VMEM((length // LANES, 3 * LANES, LANES), F32),
        pltpu.VMEM((length, LANES), F32),
    ]
    args = [qkv, mix, lse_rows, marks[0], marks[1], dmix, *fix, *smalls, *ups]
    if depth:
        rows = 4 * width // (PARTS * depth) + SMALL_ROWS
        shapes = tail + [jax.ShapeDtypeStruct((4, depth, rows, width), BF)] * 2
        scratch += [
            pltpu.VMEM((length, 3 * width), BF), pltpu.VMEM((3 * width, width), F32), pltpu.VMEM((width, width), F32),
            pltpu.VMEM((PARTS, 1, width), F32),
        ]
        args = [at, *args]
    else:
        shapes = [shape(length, 3 * width), shape(8, width, F32)] + tail
    scratch += [pltpu.VMEM(a.shape, a.dtype) for a in far] + [pltpu.SemaphoreType.DMA((len(far),))]
    return call(
        functools.partial(attention_backward_kernel, bool(fix), clear_first, depth, natural, len(smalls)),
        shapes, scratch, 22, *args, far=far, wait=wait,
    )


def norm(values):
    centred = values - jnp.mean(values, -1, keepdims=True)
    inverse = lax.rsqrt(jnp.mean(centred * centred, -1, keepdims=True) + EPSILON)
    return centred * inverse, inverse


def norm_back(upstream, scaled, inverse, gain):
    through = upstream * gain
    return inverse * (
        through
        - jnp.mean(through, -1, keepdims=True)
        - scaled * jnp.mean(through * scaled, -1, keepdims=True)
    )


def normal_terms(u):
    size = jnp.abs(u) * (1.0 / math.sqrt(2.0))
    bell = jnp.exp(-(size * size))
    s = 1.0 / (1.0 + 0.3275911 * size)
    tail = s * (0.5 * 0.254829592 + s * (0.5 * -0.284496736 + s * (0.5 * 1.421413741 + s * (0.5 * -1.453152027 + s * (0.5 * 1.061405429)))))
    tail = tail * bell
    return jnp.where(u > 0, 1.0 - tail, tail), bell * (1.0 / math.sqrt(2.0 * math.pi))


def feed_kernel(mode, pieces_at, skip_rows, clear_first, depth, *refs):
    refs = list(refs)
    take = lambda n: [refs.pop(0) for _ in range(n)]
    (at,) = take(1) if depth else (None,)
    x, mix, w_out, vectors, up_bias = take(5)
    backward = mode != "forward"
    (cot,) = take(1) if backward else (None,)
    pieces = take(len(pieces_at))
    (y,) = take(1)
    if backward:
        do_out, dr1_out, dm_out, small, up_small = take(5)
        if mode == "rows":
            n1_s, g_s, du_s, df_s = take(4)
        elif mode == "order":
            (whole,) = take(1)
        else:
            sent, kept = take(2)
    slabs, sems, z1_s, q1_s = take(4)
    if backward:
        (slope,) = take(1)
        if mode != "rows":
            n1_s, g_s, du_s, df_s, stage, out_sems = take(6)
        small[...] = jnp.zeros_like(small)
        up_small[...] = jnp.zeros_like(up_small)
    else:
        (n1_s,) = take(1)
    count, width = y.shape
    half = slabs.shape[1] // 2
    each = slabs.shape[0] // PARTS
    copies = []
    for i, (piece, begin) in enumerate(zip(pieces, pieces_at)):
        copies.append(
            pltpu.make_async_copy(
                piece.at[:, pl.ds(skip_rows, 2 * half), :], slabs.at[pl.ds(begin, piece.shape[0])], sems.at[i]
            )
        )
        copies[-1].start()

    def weights(part, lower):
        top = half if lower else 0
        return slabs[part * each : (part + 1) * each, top : top + half, :].reshape(each * half, width)

    b_out, b_down, shift_one, shift_two, gain_one, gain_two = (vectors[i : i + 1, :] for i in range(2, 8))
    r1 = x[:count, :].astype(F32) + mm(mix[:count, :], w_out[...], NT) + b_out
    z1, q1 = norm(r1)
    z1_s[...] = z1
    q1_s[...] = q1
    n1_s[...] = (z1 * gain_one + shift_one).astype(BF)
    for copy in copies:
        copy.wait()
    tile = min(256, count)

    def rows_step(i, carry):
        here = pl.ds(pl.multiple_of(i * tile, tile), tile)
        n1 = n1_s[here, :]
        acc = n1.astype(F32) + b_down
        for part in range(PARTS):
            u = mm(n1, weights(part, False), NT) + up_bias[part : part + 1, :]
            size = u.shape[1]
            cols = slice(part * size, (part + 1) * size)
            big, bell = normal_terms(u)
            g = (u * big).astype(BF)
            if backward:
                g_s[here, cols] = g
                slope[:, cols] = big + u * bell
            acc += mm(g, weights(part, True))
        z2, q2 = norm(acc)
        y[here, :] = (z2 * gain_two + shift_two).astype(BF)
        if backward:
            e = cot[here, :].astype(F32)
            if clear_first:
                e = jnp.where(lax.broadcasted_iota(jnp.int32, e.shape, 0) + i * tile == 0, 0.0, e)
            small[5:6, :] += jnp.sum(e, 0, keepdims=True)
            small[7:8, :] += jnp.sum(e * z2, 0, keepdims=True)
            dr2 = norm_back(e, z2, q2, gain_two)
            df = dr2.astype(BF)
            df_s[here, :] = df
            small[3:4, :] += jnp.sum(df.astype(F32), 0, keepdims=True)
            dn1 = dr2
            for part in range(PARTS):
                da = mm(df, weights(part, True), NT)
                size = da.shape[1]
                cols = slice(part * size, (part + 1) * size)
                du = (da * slope[:, cols]).astype(BF)
                du_s[here, cols] = du
                up_small[part : part + 1, :] += jnp.sum(du.astype(F32), 0, keepdims=True)
                dn1 += mm(du, weights(part, False))
            z1 = z1_s[here, :]
            small[4:5, :] += jnp.sum(dn1, 0, keepdims=True)
            small[6:7, :] += jnp.sum(dn1 * z1, 0, keepdims=True)
            dr1 = norm_back(dn1, z1, q1_s[here, :], gain_one)
            do = dr1.astype(BF)
            small[2:3, :] += jnp.sum(do.astype(F32), 0, keepdims=True)
            dm_out[here, :] = mm(do, w_out[...]).astype(BF)
            do_out[here, :] = do
            dr1_out[here, :] = dr1
        return carry

    lax.fori_loop(0, count // tile, rows_step, 0)
    if mode not in ("order", "spread"):
        return
    for part in range(PARTS):
        slot = part % 2
        if part > 1:
            for i in range(depth):
                pltpu.make_async_copy(stage.at[slot, i], stage.at[slot, i], out_sems.at[slot, i]).wait()
        size = g_s.shape[1] // PARTS
        cols = slice(part * size, (part + 1) * size)
        for lower, (left, right) in enumerate(((du_s, n1_s), (g_s, df_s))):
            full = mm(left[:, cols], right[...], TN).astype(BF).reshape(depth, half, width)
            stage[slot, :, lower * half : (lower + 1) * half, :] = full
        for i in range(depth):
            src, sem = stage.at[slot, i], out_sems.at[slot, i]
            if mode == "order":
                pltpu.make_async_copy(src, whole.at[i * PARTS + far_place(at, part)], sem).start()
            else:
                device = part * depth + i
                z, y_bit, x_bit, core_bit = device // PARTS, device // 4 % 2, device // 2 % 2, device % 2
                code = (at[0] ^ y_bit) + 2 * (at[1] ^ x_bit)

                @pl.when(at[2] == core_bit)
                def _():
                    pltpu.make_async_copy(src, kept.at[code, z], sem).start()

                @pl.when(at[2] != core_bit)
                def _():
                    pltpu.make_async_copy(src, sent.at[code, z], sem).start()

    for slot in range(2):
        for i in range(depth):
            pltpu.make_async_copy(stage.at[slot, i], stage.at[slot, i], out_sems.at[slot, i]).wait()


def feed(mode, x, mix, w_out, vectors, up_bias, pieces, pieces_at, cot=None, count=None, clear_first=False, skip_rows=0, depth=0, at=None, wait=()):
    width = x.shape[1]
    count = count or x.shape[0]
    hidden = PARTS * up_bias.shape[1]
    wide, high = shape(count, width), shape(count, hidden)
    rows = pieces[0].shape[1] - skip_rows
    tile = min(256, count)
    shapes = [wide]
    scratch = [
        pltpu.VMEM((2 * hidden // rows, rows, width), BF), pltpu.SemaphoreType.DMA((len(pieces),)),
        pltpu.VMEM((count, width), F32), pltpu.VMEM((count, 1), F32),
    ]
    args = [x, mix, w_out, vectors, up_bias]
    far_outs = 0
    kept = [wide, high, high, wide]
    in_vmem = [pltpu.VMEM(k.shape, BF) for k in kept]
    if mode == "forward":
        scratch.append(in_vmem[0])
    else:
        args.append(cot)
        shapes += [wide, shape(count, width, F32), wide, shape(8, width, F32), shape(*up_bias.shape, F32)]
        scratch.append(pltpu.VMEM((tile, hidden), F32))
        if mode == "rows":
            shapes += kept
        else:
            scratch += in_vmem + [pltpu.VMEM((2, depth, rows, width), BF), pltpu.SemaphoreType.DMA((2, depth))]
            out = lambda *lead: jax.ShapeDtypeStruct((*lead, rows, width), BF)
            outs = [out(PARTS * depth)] if mode == "order" else [out(4, depth), out(4, depth)]
            shapes += outs
            far_outs = len(outs)
            args = [at, *args]
    return call(
        functools.partial(feed_kernel, mode, pieces_at, skip_rows, clear_first, depth),
        shapes, scratch, 40 if count > 16 else 12, *args, far=pieces, far_outs=far_outs, wait=wait,
    )


def feed_grads_kernel(first, layout, halves, received, *refs):
    refs = list(refs)
    n1, df, g, du = (refs[i * halves : (i + 1) * halves] for i in range(4))
    refs = refs[4 * halves :]
    got = [refs.pop(0) for _ in range(received)]
    stacked = layout is None
    for index in range(refs[0].shape[0] if stacked else len(layout)):
        part = first + index
        outs = [refs[0].at[index]] if stacked else [refs.pop(0) for _ in range(layout[index])]
        size = g[0].shape[1] // PARTS
        cols = slice(part * size, (part + 1) * size)
        for lower, (left, right) in enumerate(((du, n1), (g, df))):
            full = sum(mm(a[:, cols], b[...], TN) for a, b in zip(left, right))
            at = 0
            for out in outs:
                slabs, half = out.shape[0], out.shape[1] // 2
                rows = slice(lower * half, (lower + 1) * half)
                value = full[at * half : (at + slabs) * half].reshape(slabs, half, out.shape[2])
                if received:
                    value += got[0][index, at : at + slabs, rows, :].astype(F32)
                out[:, rows, :] = value.astype(BF)
                at += slabs


def feed_grads(first, shapes, layout, n1, df, g, du, *received):
    width = n1[0].shape[1]
    outs = [jax.ShapeDtypeStruct((*lead, width), BF) for lead in shapes]
    return call(
        functools.partial(feed_grads_kernel, first, layout, len(n1), len(received)),
        outs, [], 8, *n1, *df, *g, *du, *received,
    )


def add_parts_kernel(kept, received, here, by_y, by_x, both_a, both_b):
    half = both_a.shape[0]
    for part, out in enumerate((here, by_y, by_x)):
        out[...] = kept[part] + received[part]
    both_a[...] = kept[3, :half] + received[3, :half]
    both_b[...] = kept[3, half:] + received[3, half:]


def add_parts(kept, received, wait=()):
    depth, rows, width = kept.shape[1:]
    out = lambda n: jax.ShapeDtypeStruct((n, rows, width), BF)
    shapes = [out(depth), out(depth), out(depth), out(depth // 2), out(depth // 2)]
    return call(add_parts_kernel, shapes, [], 4, kept, received, wait=wait)


def join_kernel(one, one_y, one_x, two, two_y, two_x, out):
    rows = one.shape[1]
    out[:, :rows, :] = one[...] + one_y[...] + one_x[...]
    out[:, rows:, :] = two[...] + two_y[...] + two_x[...]


def join(one, two, wait=()):
    depth, rows, width = one[0].shape
    return call(join_kernel, [jax.ShapeDtypeStruct((depth, 2 * rows, width), BF)], [], 3, *one, *two, wait=wait)[0]


def after(values, *before):
    return lax.optimization_barrier((values, before))[0]


def swap(array, axis):
    return lax.ppermute(array, axis, [(0, 1), (1, 0)])


def swaps(arrays, axis):
    return [swap(a, axis) for a in arrays]


def marks_of(lengths, segments):
    length = segments.shape[1]
    place = lax.broadcasted_iota(jnp.int32, (1, length), 1)
    keys = jnp.where(place < lengths[:, None], segments, -1)
    return segments, keys.reshape(length, 1)


class Near:
    axes = ("z", "y", "x", "core")

    def __init__(self, shards):
        self.shards = shards
        self.depth = lax.axis_size("z")
        y, x, core = (lax.axis_index(name) for name in self.axes[1:])
        self.at = jnp.stack([y, x, core])
        self.z = lax.axis_index("z")
        self.device = self.z * PARTS + y * 4 + x * 2 + core
        w_qkv, w_out, w_up = shards[:3]
        self.n_qkv, self.n_out, self.n_up = w_qkv.shape[2], w_out.shape[2], w_up.shape[2]
        half = self.depth // 2
        own = [(0, 0), (1, 0), (2, 0), (3, 0), (3, half)]
        self.slabs = own + [(part + 4, first) for part, first in own]

    def slab_pair(self, index):
        w_qkv, w_out, w_up, w_down, biases, gains, up_bias = (s[index] for s in self.shards)
        width = w_qkv.shape[0]
        natural = lax.dynamic_update_slice(
            jnp.zeros((8, width), BF), jnp.concatenate([biases, gains], 0), (0, self.device * self.n_out)
        )
        line = lax.dynamic_update_slice(jnp.zeros((8, width), BF), up_bias[None], (0, self.z * self.n_up))
        attention = jnp.concatenate([w_qkv.T, w_out.T, natural, line], 0)
        return attention, jnp.concatenate([w_up.T, w_down], 0)

    def along_z(self, slab):
        return lax.all_gather(slab, "z", axis=0, tiled=False)

    def near(self, here):
        return [here, swap(here, "y"), swap(here, "x")]

    def diagonal(self, near):
        half = self.depth // 2
        return [swap(near[1][:half], "x"), swap(near[2][half:], "y")]

    def attend(self, x, marks, pieces):
        slabs = self.slabs if len(pieces) > 1 else []
        out = attention_forward(x, marks, pieces, self.at, slabs, self.depth, self.n_up)
        return dict(zip(("x", "qkv", "mix", "lse", "wt", "wt_out", "small", "up_bias"), [x, *out]))

    def feed(self, mode, kept, pieces, cot, count=None, clear_first=False, wait=()):
        if len(pieces) > 1:
            pieces_at = [part * self.depth + first for part, first in self.slabs]
        else:
            pieces_at = [0]
        grads = mode != "rows"
        out = feed(
            mode, kept["x"], kept["mix"], kept["wt_out"], kept["small"], kept["up_bias"], pieces, pieces_at,
            cot, count, clear_first, pieces[0].shape[1] - 2 * self.n_up,
            self.depth if grads else 0, self.at if grads else None, wait,
        )
        last = {"rows": ("n1", "g", "du", "df"), "order": ("all",), "spread": ("sent", "kept")}[mode]
        return dict(zip(("y", "do", "dr1", "dm", "small", "up") + last, out))

    def reduce_diagonal(self, both):
        return [swap(both[0], "x"), swap(both[1], "y")]

    def add_diagonal(self, by_y, by_x, got):
        half = self.depth // 2
        return [by_y.at[:half].add(got[0]), by_x.at[half:].add(got[1])]

    def reduce_near(self, added):
        return [swap(added[0], "y"), swap(added[1], "x")]

    def reduce_z(self, here, got):
        return lax.psum_scatter(here + got[0] + got[1], "z", scatter_dimension=0, tiled=False)

    def attend_back(self, kept, marks, back, fix, clear_first, natural, wait=()):
        smalls, ups = [f["small"] for f in [back, *fix]], [f["up"] for f in [back, *fix]]
        return attention_backward(
            kept["qkv"], kept["mix"], kept["lse"], marks, back["dm"], [f[n] for f in fix for n in ("dm", "dr1", "do")],
            [kept["wt"], back["dr1"], kept["x"], back["do"]], clear_first, self.depth, self.at, smalls, ups, natural, wait,
        )

    def attention_outs(self, total, natural):
        total = total.astype(F32)
        n_qkv, n_out, n_up = self.n_qkv, self.n_out, self.n_up
        small = total[n_qkv + n_out :]
        own = lax.dynamic_slice(small, (0, self.device * n_out), (8, n_out))
        up = lax.dynamic_slice(small, (8, (self.device % self.depth if natural else self.z) * n_up), (1, n_up))[0]
        return total[:n_qkv].T, total[n_qkv : n_qkv + n_out].T, own[:6], own[6:], up

    def first_row_terms(self, fix):
        width = fix["n1"].shape[1]
        rows = jnp.stack([fix["n1"][0], fix["df"][0]]).reshape(1, 2 * width)
        table = jnp.stack([fix["du"][0].reshape(PARTS, self.depth, self.n_up), fix["g"][0].reshape(PARTS, self.depth, self.n_up)], 2)
        table = table.reshape(1, PARTS, -1)
        for axis in ("core", "x", "y"):
            n, far = table.shape[0], table.shape[1] // 2
            flat = jnp.concatenate([rows, table[:, far:].reshape(n, -1)], 1)
            got = swap(flat, axis)
            rows = jnp.concatenate([rows, got[:, : 2 * width]], 0)
            table = jnp.concatenate([table[:, :far], got[:, 2 * width :].reshape(n, far, -1)], 0)
        n = rows.shape[0]
        flat = jnp.concatenate([rows, table.reshape(n, -1)], 1)
        step = 1
        while step < self.depth:
            pairs = [(i, i ^ step) for i in range(self.depth)]
            flat = jnp.concatenate([flat, lax.ppermute(flat, "z", pairs)], 0)
            step *= 2
        own = flat[:, 2 * width :].reshape(flat.shape[0], self.depth, 2, self.n_up)
        own = lax.dynamic_index_in_dim(own, self.z, 1, keepdims=False)
        up = mm(own[:, 0], flat[:, :width], TN)
        down = mm(own[:, 1], flat[:, width : 2 * width], TN)
        return up, down


def near_body(tokens, skip_tokens, cot_first, cot_second, *rest):
    *shards, lengths, segments = rest
    link = Near(shards)
    marks = marks_of(lengths, segments)
    length = segments.shape[1]
    is_first = lax.broadcasted_iota(jnp.int32, (length, 1), 0) == 0

    slab_a1, slab_m1 = link.slab_pair(0)
    a1 = link.along_z(slab_a1)
    m1 = link.along_z(slab_m1)
    b2 = [lax.all_gather(after(jnp.concatenate(link.slab_pair(1), 0), a1), link.axes, axis=0, tiled=False)]
    a1 = link.near(a1)
    a1 += link.diagonal(a1)
    m1 = link.near(after(m1, a1[:3]))
    a1 += swaps(a1, "core")
    one = link.attend(*after((tokens, marks, a1), m1))
    m1 += link.diagonal(m1)
    m1 += swaps(m1, "core")
    back_one = link.feed("order", one, m1, cot_first, None, True)
    sum_m1 = lax.psum_scatter(back_one["all"], link.axes, scatter_dimension=0, tiled=False)
    out_first = back_one["y"]
    second_in = jnp.where(is_first, out_first, skip_tokens)
    two = link.attend(second_in, marks, b2)
    back_two = link.feed("spread", two, b2, cot_second)
    received_m2 = swap(back_two["sent"], "core")
    grad_skip, first2, sent_a2, kept_a2 = link.attend_back(two, marks, back_two, [], True, True)
    kept_m2, received_m2, sent_a2, kept_a2 = after((back_two["kept"], received_m2, sent_a2, kept_a2), first2)
    received_a2 = swap(sent_a2, "core")
    kept_m2 = add_parts(kept_m2, received_m2)
    got_m2 = link.reduce_diagonal(kept_m2[3:])
    kept_a2 = add_parts(kept_a2, received_a2)
    got_a2 = link.reduce_diagonal(kept_a2[3:])
    upstream = jnp.where(is_first[:16], cot_first[:16].astype(F32) + first2, 0.0)
    fix = link.feed("rows", one, m1, after(upstream, kept_m2, kept_a2), 16)
    kept_m2, got_m2, kept_a2, got_a2 = after((kept_m2, got_m2, kept_a2, got_a2), fix["y"])
    added_m2 = link.add_diagonal(*kept_m2[1:3], got_m2)
    got_m2 = link.reduce_near(added_m2)
    grad_tokens, _, sent_a1, kept_a1 = link.attend_back(
        one, marks, *after((back_one, [fix]), added_m2), False, False
    )
    kept_m2, got_m2, kept_a2, got_a2, sent_a1, sum_m1 = after(
        (kept_m2, got_m2, kept_a2, got_a2, sent_a1, sum_m1), kept_a1
    )
    received_a1 = swap(sent_a1, "core")
    sum_m2 = link.reduce_z(kept_m2[0], got_m2)
    added_a2 = link.add_diagonal(*kept_a2[1:3], got_a2)
    got_a2 = link.reduce_near(added_a2)
    kept_a1 = add_parts(*after((kept_a1, received_a1), added_a2))
    got_a1 = link.reduce_diagonal(kept_a1[3:])
    got_a1 = link.reduce_near(link.add_diagonal(*kept_a1[1:3], got_a1))
    fix = after(fix, kept_a1)
    both = join([kept_a1[0], *got_a1], [kept_a2[0], *got_a2], [sum_m2])
    both = lax.psum_scatter(both, "z", scatter_dimension=0, tiled=False)
    sum_a1, sum_a2 = both[: both.shape[0] // 2], both[both.shape[0] // 2 :]

    n_up = link.n_up
    up_fix, down_fix = link.first_row_terms(fix)
    sum_m1, sum_m2 = sum_m1.astype(F32), sum_m2.astype(F32)
    outs = [link.attention_outs(sum_a1, False), link.attention_outs(sum_a2, True)]
    pair = lambda i: jnp.stack([outs[0][i], outs[1][i]])
    return (
        out_first, back_two["y"], grad_tokens, grad_skip,
        pair(0), pair(1),
        jnp.stack([(sum_m1[:n_up] + up_fix).T, sum_m2[:n_up].T]),
        jnp.stack([sum_m1[n_up:] + down_fix, sum_m2[n_up:]]),
        pair(2), pair(3), pair(4),
    )


def far_body(tokens, skip_tokens, cot_first, cot_second, *rest):
    *shards, lengths, segments = rest
    axes = ("wide", "narrow")
    devices = lax.axis_size("wide") * lax.axis_size("narrow")
    marks = marks_of(lengths, segments)
    length, width = tokens.shape
    is_first = lax.broadcasted_iota(jnp.int32, (length, 1), 0) == 0
    gather = lambda a: lax.all_gather(a, axes, axis=0, tiled=True)
    scatter = lambda a: lax.psum_scatter(a, axes, scatter_dimension=0, tiled=True)

    def fetch(index):
        w_qkv, w_out, w_up, w_down, biases, gains, up_bias = (s[index] for s in shards)
        small = gather(jnp.concatenate([biases, gains], 0).T).T.astype(F32)
        up, down = (gather(w).reshape(PARTS, -1, width) for w in (w_up.T, w_down))
        both = jnp.concatenate([up, down], 1)
        return (
            gather(w_qkv.T), gather(w_out.T), small, gather(up_bias).astype(F32).reshape(PARTS, -1),
            [both],
        )

    def forward(x, weights):
        wt, wt_out, small, up_bias, pieces = weights
        qkv, mix, lse = attention_forward(x, marks, (wt, small))
        return (qkv, mix, lse), feed("forward", x, mix, wt_out, small, up_bias, pieces, [0])[0]

    def backward(x, weights, kept, cot, clear_first):
        wt, wt_out, small, up_bias, pieces = weights
        qkv, mix, lse = kept
        y, do, dr1, dm, sums, up_sums, n1, g, du, df = feed("rows", x, mix, wt_out, small, up_bias, pieces, [0], cot)
        dqkv, more, dx, first = attention_backward(qkv, mix, lse, marks, dm, [], [wt, dr1], clear_first)
        rows = 2 * up_bias.shape[1]
        lists = [[n1], [df], [g], [du]]
        parts = jnp.concatenate([feed_grads(i, [(4, 1, rows)], None, *lists)[0][:, 0] for i in (0, 4)], 0)
        up, down = (p.reshape(-1, width) for p in (parts[:, : rows // 2], parts[:, rows // 2 :]))
        sums = scatter((sums + more).T).T
        grads = (
            scatter(mm(dqkv, x, TN).astype(BF)).astype(F32).T,
            scatter(mm(do, mix, TN).astype(BF)).astype(F32).T,
            scatter(up).astype(F32).T,
            scatter(down).astype(F32),
            sums[:6], sums[6:], scatter(up_sums.reshape(-1)),
        )
        return y, dx, first, grads

    one, two = fetch(0), fetch(1)
    kept_one, out_first = forward(tokens, one)
    second_in = jnp.where(is_first, out_first, skip_tokens)
    kept_two, _ = forward(second_in, two)
    out_second, grad_skip, first, grads_two = backward(second_in, two, kept_two, cot_second, True)
    first = jnp.concatenate([first, jnp.zeros((length - first.shape[0], width), F32)], 0)
    upstream = cot_first.astype(F32) + jnp.where(is_first, first, 0.0)
    _, grad_tokens, _, grads_one = backward(tokens, one, kept_one, upstream, False)
    return (out_first, out_second, grad_tokens, grad_skip, *(jnp.stack(p) for p in zip(grads_one, grads_two)))


def solution(mesh):
    wide, narrow = mesh.shape["wide"], mesh.shape["narrow"]
    if narrow == 4 and wide % 4 == 0:
        mesh = Mesh(mesh.devices.reshape(wide // 2, 2, 2, 2), Near.axes)
        body, every = near_body, Near.axes
    else:
        body, every = far_body, ("wide", "narrow")
    rows, last, middle = P(every, None), P(None, None, every), P(None, every, None)
    return jax.shard_map(
        body,
        mesh=mesh,
        in_specs=(
            rows, rows, rows, rows, last, last, last, middle, last, last, P(None, every), P(every), rows,
        ),
        out_specs=(rows, rows, rows, rows, last, last, last, middle, last, last, P(None, every)),
        check_vma=False,
    )
```
